256 devices in a mesh: replica: 4 (over y), fsdp: 32 (over x, z), tensor: 2 (over core).
Axes of the slice: x: 4, y: 4, z: 8, core: 2. Of those that a mesh axis runs over, the one named last changes fastest.
Arguments:
- weight: bfloat16 [14336, 4096], P('fsdp', 'tensor'), may hold values from -0.046875 to 0.046875
- momentum: float32 [4, 14336, 4096], P('replica', 'fsdp', 'tensor'), may hold values from -6 to 6
- grad: bfloat16 [4, 14336, 4096], P('replica', 'fsdp', 'tensor'), may hold values from -270 to 270
- basis: float32 [4096, 256], P('tensor', 'fsdp'), may hold values from -0.09375 to 0.09375
Outputs:
- new_weight: bfloat16 [14336, 4096], P('fsdp', 'tensor')
- new_momentum: float32 [4, 14336, 4096], P('replica', 'fsdp', 'tensor')
- new_basis: float32 [4096, 256], P('tensor', 'fsdp')
The draws below stay inside these ranges and needn't reach their ends.
All inputs are finite; a program needn't handle non-finite values.
Results may differ from the reference program's by a relative error of at most 0.001.
Values sent between devices are 32-bit elements; how exact they have to be, the bound alone decides.
A program may use at most 64 MiB of HBM per device.

```python
import math
import jax
import jax.numpy as jnp
from jax import lax

ROWS = 14336
COLS = 4096
RANK = 256
REPS = 4


def draw_grad(key, part):
    key = jax.random.fold_in(key, 7)
    row_key, col_key, base_key = jax.random.split(key, 3)
    row_trend = 1.0 + 2.0 * jnp.arange(ROWS, dtype=jnp.float32) / (ROWS - 1)
    col_trend = 1.0 + 2.0 * jnp.arange(COLS, dtype=jnp.float32) / (COLS - 1)
    row_scale = jnp.exp(jax.random.uniform(row_key, (ROWS,), jnp.float32, 0.0, math.log(10.0))) * row_trend
    col_scale = jnp.exp(jax.random.uniform(col_key, (COLS,), jnp.float32, 0.0, math.log(10.0))) * col_trend
    values = jax.random.truncated_normal(base_key, -6.0, 6.0, (REPS, ROWS, COLS), jnp.float32)
    scaled = values * row_scale[None, :, None] * col_scale[None, None, :] / 20.0
    return scaled.astype(jnp.bfloat16)


def level_of(key, extent, shards, least, top_value):
    loudness = 1.0
    for axis_at, parts in shards:
        steps = jax.random.uniform(jax.random.fold_in(jax.random.fold_in(key, 6), axis_at), (parts,), jnp.float32, least / len(shards), top_value / len(shards))
        loudness = loudness * jnp.repeat(jnp.exp(steps), extent[axis_at] // parts).reshape((-1,) + (1,) * (len(extent) - 1 - axis_at))
    return loudness


def bell_draw(own_key, shape, scale, bound, shards=(), held_as=jnp.bfloat16):
    level = level_of(own_key, shape, shards, -0.22, 0.18) if shards else 1.0
    entries = jax.random.normal(own_key, shape, jnp.float32) * scale * level
    return jnp.minimum(jnp.maximum(entries, -bound), bound).astype(held_as)


def setup_inputs(seed: int = 0) -> dict:
    streams_of = jax.random.split(jax.random.key(seed), 5)
    weight = bell_draw(streams_of[0], (ROWS, COLS), ROWS ** -0.5, 0.046875, ((0, 32), (1, 2)))
    momentum = bell_draw(streams_of[1], (REPS, ROWS, COLS), 1.0, 6.0, ((0, 4), (1, 32), (2, 2)), jnp.float32)
    grad = draw_grad(jax.random.fold_in(streams_of[4], 71), 0)
    basis = bell_draw(streams_of[3], (COLS, RANK), COLS ** -0.5, 0.09375, ((0, 2), (1, 32)), jnp.float32)
    return dict(weight=weight, momentum=momentum, grad=grad, basis=basis)


def product(first, second):
    return jnp.dot(first, second, precision=lax.Precision.HIGHEST)

def reference(weight, momentum, grad, basis):
    buffer = momentum + grad.astype(jnp.float32)
    left_factor = jnp.einsum('kmn,nr->mr', buffer, basis, precision=lax.Precision.HIGHEST) / REPS
    gram_matrix = product(left_factor.T, left_factor)
    lower_factor = jnp.linalg.cholesky(gram_matrix)
    ortho_factor = lax.linalg.triangular_solve(lower_factor, left_factor, left_side=False, lower=True, transpose_a=True)
    right_factor = jnp.einsum('kmn,mr->nr', buffer, ortho_factor, precision=lax.Precision.HIGHEST) / REPS
    column_norms = jnp.sqrt(lax.optimization_barrier(jnp.sum(right_factor * right_factor, axis=0, keepdims=True)) + 1e-06)
    new_basis = right_factor / column_norms
    new_momentum = buffer - 0.05 * product(ortho_factor, right_factor.T)[None]
    scale_factor = 0.1 * math.sqrt(ROWS / COLS)
    new_weight = (weight.astype(jnp.float32) - scale_factor * product(ortho_factor, new_basis.T)).astype(jnp.bfloat16)
    return (new_weight, new_momentum, new_basis)
```

```python
import math

import jax
import jax.numpy as jnp
from jax import lax
from jax.experimental import pallas as pl
from jax.experimental.pallas import tpu as pltpu
from jax.sharding import PartitionSpec as P

ROWS = 14336
COLS = 4096
RANK = 256
NX, NY, NZ = 4, 4, 8
MB = 448
NB = 2048
HALF = NB // 2
CH = 256
BLK = 64
MESH = pl.DeviceIdType.MESH
HIGH = lax.Precision.HIGHEST
F32 = jnp.float32

COUNT = {}
TOTAL = 0
for _name, _n in (
    ("ax", 3), ("az", 28), ("bz", 7), ("bx", 3),
    ("lc", 1), ("ly", 3), ("ly2", 3), ("lc2", 1),
    ("gx", 3), ("gz", 7), ("gx2", 3), ("gy2", 3), ("gc2", 1),
    ("wa1", 3), ("wb1", 12), ("wa2", 3), ("wb2", 3), ("w3", 7),
    ("wz", 7), ("wa5", 3), ("wb5", 3), ("wa6", 3), ("wb6", 3), ("n", 1),
):
    COUNT[_name] = TOTAL
    TOTAL += _n


def dot(a, b, dims):
    return lax.dot_general(a, b, (dims, ((), ())), precision=HIGH, preferred_element_type=F32)


def nn(a, b):
    return dot(a, b, ((1,), (0,)))


def nt(a, b):
    return dot(a, b, ((1,), (1,)))


def tn(a, b):
    return dot(a, b, ((0,), (0,)))


def pivots(done, t):
    top, rest = t[0:8], t[8:]
    below = lax.broadcasted_iota(jnp.int32, (8, 1), 0)
    left = lax.broadcasted_iota(jnp.int32, (BLK - 8, 1), 0) < BLK - 8 - 8 * done
    for k in range(8):
        rs = lax.rsqrt(top[k : k + 1, k : k + 1])
        row = top[k : k + 1, :] * rs
        col = jnp.where(below > k, top[:, k : k + 1] * rs, 0.0)
        low = jnp.where(left, rest[:, k : k + 1] * rs, 0.0)
        top = jnp.where(below == k, row, top - col * row)
        rest = rest - low * row
    return pltpu.roll(jnp.concatenate([rest, top], axis=0), 2 * BLK - 8, 1)


def chol_block(b, a_ref, li_ref):
    r0 = BLK * b
    w0 = 2 * BLK * (b // 2)
    odd = b % 2
    lane = lax.broadcasted_iota(jnp.int32, (BLK, 2 * BLK), 1)
    row = lax.broadcasted_iota(jnp.int32, (BLK, 2 * BLK), 0)
    t = a_ref[r0 : r0 + BLK, w0 : w0 + 2 * BLK]
    if odd:
        t = pltpu.roll(t, BLK, 1)
    t = jnp.where(lane < BLK, t, jnp.where(lane - BLK == row, 1.0, 0.0))
    t = lax.fori_loop(0, BLK // 8, pivots, t)
    inv = jnp.where(lane < BLK, t, 0.0)
    if odd:
        inv = pltpu.roll(inv, BLK, 1)
    u = nn(inv, a_ref[w0 : w0 + 2 * BLK, :])
    ul = nn(inv, li_ref[w0 : w0 + 2 * BLK, :])
    if r0 + BLK < RANK:
        rows = lax.broadcasted_iota(jnp.int32, (RANK, 1), 0)
        a_ref[...] = a_ref[...] - tn(u, u)
        li_ref[...] = jnp.where(rows >= r0 + BLK, li_ref[...] - tn(u, ul), li_ref[...])
    li_ref[r0 : r0 + BLK, :] = ul


def kernel(
    mom_hbm, grad_hbm, bas_in,
    right_out, ortho_out, norm_out, newb_out,
    buf, gra, bas, lpart, lrc, lry, left, leftT, gpart, grx, grz, gram, linv,
    w, ra1, rb1, sa1, sb1, ra2, rb2, s2, r3, wf, nown, nrec,
    lsem, ssem, rsem,
):
    y = lax.axis_index("replica")
    f = lax.axis_index("fsdp")
    core = lax.axis_index("tensor")
    x, z = f // NZ, f % NZ

    def xp(d):
        return (y, lax.rem(x + d + NX, NX) * NZ + z, core)

    def yp(d):
        return (lax.rem(y + d + NY, NY), f, core)

    def zp(d):
        return (y, x * NZ + lax.rem(z + d + NZ, NZ), core)

    cp = (y, f, 1 - core)

    load_m = pltpu.make_async_copy(mom_hbm, buf, lsem.at[0])
    load_g = pltpu.make_async_copy(grad_hbm, gra, lsem.at[1])
    load_m.start()
    load_g.start()

    sent = []

    def make(src, dst, name, n, dev):
        k = COUNT[name] + n
        return pltpu.make_async_remote_copy(
            src_ref=src, dst_ref=dst, send_sem=ssem.at[k], recv_sem=rsem.at[k],
            device_id=dev, device_id_type=MESH,
        )

    def send(*args):
        copy = make(*args)
        copy.start()
        sent.append(copy)
        return copy

    bas[0, x, z] = bas_in[:, :HALF]
    bas[1, x, z] = bas_in[:, HALF:]

    barrier = pltpu.get_barrier_semaphore()
    peers = [xp(d) for d in range(1, NX)] + [yp(d) for d in range(1, NY)]
    peers += [zp(d) for d in range(1, NZ)] + [cp]
    for dev in peers:
        pl.semaphore_signal(barrier, inc=1, device_id=dev, device_id_type=MESH)
    pl.semaphore_wait(barrier, len(peers))

    def ring(way, step, i):
        piece = bas.at[0, lax.rem(x - i + NX, NX), lax.rem(z - way * (step - 1) + NZ, NZ)]
        return send(piece, piece, "az", (16 if way < 0 else 0) + (step - 1) * 4 + i, zp(way))

    hops = {}
    mine = bas.at[0, x, z]
    ax = [send(mine, mine, "ax", d - 1, xp(d)) for d in range(1, NX)]
    hops[1, 1, 0] = ring(1, 1, 0)
    hops[-1, 1, 0] = ring(-1, 1, 0)
    mine = bas.at[1, x, z]
    bz = [send(mine, mine, "bz", d - 1, zp(d)) for d in range(1, NZ)]
    for i in range(1, NX):
        ax[i - 1].wait_recv()
        hops[1, 1, i] = ring(1, 1, i)
        hops[-1, 1, i] = ring(-1, 1, i)
    for copy in bz:
        copy.wait_recv()
    mine = bas.at[1, x]
    bx = [send(mine, mine, "bx", d - 1, xp(d)) for d in range(1, NX)]
    for step in range(2, 5):
        for i in range(NX):
            for way in (1, -1):
                if (way, step - 1, i) in hops:
                    hops.pop((way, step - 1, i)).wait_recv()
                if way == 1 or step < 4:
                    hops[way, step, i] = ring(way, step, i)
    load_m.wait()
    load_g.wait()
    for r in range(0, MB, 64):
        rows = slice(r, r + 64)
        buf[rows, :] = buf[rows, :] + gra[rows, :].astype(F32)
    for copy in list(hops.values()) + bx:
        copy.wait_recv()

    lpart[...] = jnp.zeros_like(lpart)
    for h in range(2):

        @pl.loop(0, HALF // CH)
        def _(c):
            at = pl.multiple_of(c * CH, CH)
            part = bas[h, :, :, :, pl.ds(at, CH)].reshape(RANK, CH)
            lpart[...] += nt(buf[:, pl.ds(pl.multiple_of(h * HALF + at, CH), CH)], part)

    hm, qm = MB // 2, MB // 8
    own = pl.multiple_of(core * hm, 8)
    other = pl.multiple_of((1 - core) * hm, 8)
    lc = send(lpart.at[pl.ds(other, hm)], lrc, "lc", 0, cp)
    lc.wait_recv()
    lpart[pl.ds(own, hm), :] = lpart[pl.ds(own, hm), :] + lrc[...]

    def quarter(q):
        return pl.ds(pl.multiple_of(own + q * qm, 8), qm)

    ly = [
        send(lpart.at[quarter(lax.rem(y + d, NY))], lry.at[d - 1], "ly", d - 1, yp(d))
        for d in range(1, NY)
    ]
    for copy in ly:
        copy.wait_recv()
    left[quarter(y), :] = (lpart[quarter(y), :] + lry[0] + lry[1] + lry[2]) * 0.25
    mine = left.at[quarter(y)]
    ly2 = [send(mine, mine, "ly2", d - 1, yp(d)) for d in range(1, NY)]
    for copy in ly2:
        copy.wait_recv()
    mine = left.at[pl.ds(own, hm)]
    lc2 = send(mine, mine, "lc2", 0, cp)
    lc2.wait_recv()

    leftT[...] = left[...].T
    gpart[...] = nt(leftT[...], leftT[...])
    g0 = core * 128 + y * 32

    def grows(base, n):
        return pl.ds(pl.multiple_of(base, 8), n)

    gx = [
        send(gpart.at[grows(g0 + 8 * lax.rem(x + d, NX), 8)], grx.at[d - 1], "gx", d - 1, xp(d))
        for d in range(1, NX)
    ]

    wa1, wb1 = [], []

    def product(h, g):
        at = pl.multiple_of(h * HALF + g * CH, CH)
        w[h, g] = nn(leftT[...], buf[:, pl.ds(at, CH)])

    def yrows(q):
        return pl.ds(pl.multiple_of(q * 64, 64), 64)

    for i in (1, 2, 3, 0):
        g = lax.rem(x + i, NX)
        product(0, g)
        if i:
            wa1.append(send(w.at[0, g], ra1.at[i - 1], "wa1", i - 1, xp(i)))
        product(1, i)
        for d in range(1, NY):
            wb1.append(
                send(w.at[1, i, yrows(lax.rem(y + d, NY))], rb1.at[d - 1, i], "wb1",
                     (d - 1) * 4 + i, yp(d))
            )

    for copy in gx:
        copy.wait_recv()
    mine = grows(g0 + 8 * x, 8)
    grz[z] = gpart[mine, :] + grx[0] + grx[1] + grx[2]
    gz = [send(grz.at[z], grz.at[z], "gz", d - 1, zp(d)) for d in range(1, NZ)]
    for copy in gz:
        copy.wait_recv()
    total = grz[0]
    for k in range(1, NZ):
        total = total + grz[k]
    gram[mine, :] = total
    part = gram.at[mine]
    gx2 = [send(part, part, "gx2", d - 1, xp(d)) for d in range(1, NX)]
    for copy in gx2:
        copy.wait_recv()
    part = gram.at[grows(g0, 32)]
    gy2 = [send(part, part, "gy2", d - 1, yp(d)) for d in range(1, NY)]
    for copy in gy2:
        copy.wait_recv()
    part = gram.at[grows(core * 128, 128)]
    gc2 = send(part, part, "gc2", 0, cp)
    gc2.wait_recv()

    for copy in wa1:
        copy.wait_recv()
    sa1[...] = w[0, x] + ra1[0] + ra1[1] + ra1[2]
    wa2 = [
        send(sa1.at[yrows(lax.rem(y + d, NY))], ra2.at[d - 1], "wa2", d - 1, yp(d))
        for d in range(1, NY)
    ]
    for copy in wb1:
        copy.wait_recv()
    for g in range(NX):
        sb1[g] = w[1, g, yrows(y), :] + rb1[0, g] + rb1[1, g] + rb1[2, g]
    wb2 = [
        send(sb1.at[lax.rem(x + d, NX)], rb2.at[d - 1], "wb2", d - 1, xp(d)) for d in range(1, NX)
    ]

    for copy in gx2 + gy2 + [gc2]:
        copy.wait_send()
    sent[:] = [copy for copy in sent if not any(copy is c for c in gx2 + gy2 + [gc2])]
    rows = lax.broadcasted_iota(jnp.int32, (RANK, RANK), 0)
    cols = lax.broadcasted_iota(jnp.int32, (RANK, RANK), 1)
    linv[...] = jnp.where(rows == cols, 1.0, 0.0)
    chol_block(0, gram, linv)

    for copy in wa2 + wb2:
        copy.wait_recv()
    s2[0] = sa1[yrows(y), :] + ra2[0] + ra2[1] + ra2[2]
    s2[1] = sb1[x] + rb2[0] + rb2[1] + rb2[2]

    def zrows(q):
        return pl.ds(pl.multiple_of(q * 8, 8), 8)

    w3 = [
        send(s2.at[:, zrows(lax.rem(z + d, NZ))], r3.at[d - 1], "w3", d - 1, zp(d))
        for d in range(1, NZ)
    ]
    chol_block(1, gram, linv)

    for copy in w3:
        copy.wait_recv()
    total = s2[:, zrows(z), :]
    for k in range(NZ - 1):
        total = total + r3[k]
    mine = pl.ds(pl.multiple_of(y * 64 + z * 8, 8), 8)
    wf[:, x, mine, :] = total
    part = wf.at[:, x, mine]
    wz = [send(part, part, "wz", d - 1, zp(d)) for d in range(1, NZ)]
    for copy in wz:
        copy.wait_recv()
    part = wf.at[0, x, yrows(y)]
    wa5 = [send(part, part, "wa5", d - 1, yp(d)) for d in range(1, NY)]
    part = wf.at[1, x, yrows(y)]
    wb5 = [send(part, part, "wb5", d - 1, xp(d)) for d in range(1, NX)]
    chol_block(2, gram, linv)
    for copy in wa5 + wb5:
        copy.wait_recv()
    part = wf.at[0, x]
    wa6 = [send(part, part, "wa6", d - 1, xp(d)) for d in range(1, NX)]
    part = wf.at[1, :, yrows(y)]
    wb6 = [send(part, part, "wb6", d - 1, yp(d)) for d in range(1, NY)]
    chol_block(3, gram, linv)
    ortho_out[...] = nt(left[...], linv[...])
    for copy in wa6 + wb6:
        copy.wait_recv()

    nown[...] = jnp.zeros_like(nown)
    for h in range(2):

        @pl.loop(0, NX)
        def _(g):
            part = nn(linv[...], wf[h, g] * 0.25)
            right_out[:, pl.ds(pl.multiple_of(h * HALF + g * CH, CH), CH)] = part
            sq = part * part
            nown[...] += sq[:, :128] + sq[:, 128:]

    ns = send(nown, nrec, "n", 0, cp)
    ns.wait_recv()
    norms = jnp.sqrt(jnp.sum(nown[...] + nrec[...], axis=1, keepdims=True) + 1e-06)
    norm_out[...] = jnp.broadcast_to(norms, (RANK, 128))
    mine = pl.ds(pl.multiple_of(f * 8, 8), 8)
    newb_out[...] = right_out[mine, :] / norm_out[mine, 0:1]

    for copy in sent:
        copy.wait_send()


def factors(momentum, grad, basis_t):
    v = pltpu.VMEM
    any_ = pl.BlockSpec(memory_space=pl.ANY)
    vm = pl.BlockSpec(memory_space=pltpu.VMEM)
    return pl.pallas_call(
        kernel,
        out_shape=(
            jax.ShapeDtypeStruct((RANK, NB), F32),
            jax.ShapeDtypeStruct((MB, RANK), F32),
            jax.ShapeDtypeStruct((RANK, 128), F32),
            jax.ShapeDtypeStruct((8, NB), F32),
        ),
        in_specs=[any_, any_, vm],
        out_specs=(vm, vm, vm, vm),
        scratch_shapes=[
            v((MB, NB), F32), v((MB, NB), jnp.bfloat16), v((2, NX, NZ, 8, HALF), F32),
            v((MB, RANK), F32), v((MB // 2, RANK), F32), v((3, MB // 8, RANK), F32),
            v((MB, RANK), F32), v((RANK, MB), F32),
            v((RANK, RANK), F32), v((3, 8, RANK), F32), v((NZ, 8, RANK), F32),
            v((RANK, RANK), F32), v((RANK, RANK), F32),
            v((2, NX, RANK, CH), F32), v((3, RANK, CH), F32), v((3, NX, 64, CH), F32),
            v((RANK, CH), F32), v((NX, 64, CH), F32),
            v((3, 64, CH), F32), v((3, 64, CH), F32), v((2, 64, CH), F32),
            v((7, 2, 8, CH), F32), v((2, NX, RANK, CH), F32),
            v((RANK, 128), F32), v((RANK, 128), F32),
            pltpu.SemaphoreType.DMA((2,)),
            pltpu.SemaphoreType.DMA((TOTAL,)),
            pltpu.SemaphoreType.DMA((TOTAL,)),
        ],
        compiler_params=pltpu.CompilerParams(
            collective_id=0, has_side_effects=True, vmem_limit_bytes=48 * 1024 * 1024
        ),
        name="factors",
    )(momentum, grad, basis_t)


def update_kernel(ortho, right, norm, mom, grad, weight, new_mom, new_w):
    scale = 0.1 * math.sqrt(ROWS / COLS)
    part = right[...]
    buffer = mom[...] + grad[...].astype(F32)
    new_mom[...] = buffer - 0.05 * nn(ortho[...], part)
    delta = nn(ortho[...], part / norm[:, 0:1])
    new_w[...] = (weight[...].astype(F32) - scale * delta).astype(jnp.bfloat16)


def update(ortho, right, norm, momentum, grad, weight):
    cols = pl.BlockSpec((MB, CH), lambda i: (0, i))
    return pl.pallas_call(
        update_kernel,
        grid=(NB // CH,),
        out_shape=(
            jax.ShapeDtypeStruct((MB, NB), F32),
            jax.ShapeDtypeStruct((MB, NB), jnp.bfloat16),
        ),
        in_specs=[
            pl.BlockSpec((MB, RANK), lambda i: (0, 0)),
            pl.BlockSpec((RANK, CH), lambda i: (0, i)),
            pl.BlockSpec((RANK, 128), lambda i: (0, 0)),
            cols, cols, cols,
        ],
        out_specs=(cols, cols),
        compiler_params=pltpu.CompilerParams(vmem_limit_bytes=32 * 1024 * 1024),
        name="update",
    )(ortho, right, norm, momentum, grad, weight)


def body(weight, momentum, grad, basis):
    right, ortho, norm, new_basis_t = factors(momentum[0], grad[0], basis.T)
    new_momentum, new_weight = update(ortho, right, norm, momentum[0], grad[0], weight)
    return new_weight, new_momentum[None], new_basis_t.T


def solution(mesh):
    return jax.shard_map(
        body,
        mesh=mesh,
        in_specs=(
            P("fsdp", "tensor"),
            P("replica", "fsdp", "tensor"),
            P("replica", "fsdp", "tensor"),
            P("tensor", "fsdp"),
        ),
        out_specs=(P("fsdp", "tensor"), P("replica", "fsdp", "tensor"), P("tensor", "fsdp")),
        check_vma=False,
    )
```

```python
import math

import jax
import jax.numpy as jnp
from jax import lax
from jax.experimental import pallas as pl
from jax.experimental.pallas import tpu as pltpu
from jax.sharding import PartitionSpec as P

ROWS = 14336
COLS = 4096
RANK = 256
NX, NY, NZ = 4, 4, 8
MB = 448
NB = 2048
HALF = NB // 2
CH = 256
LN = CH // 2
BLK = 64
MESH = pl.DeviceIdType.MESH
HIGH = lax.Precision.HIGHEST
F32 = jnp.float32
BF16 = jnp.bfloat16
SCHEDULE = (1, 2, 2, 2, 2, 2)

COUNT, COUNTS = {}, {}
TOTAL = 0
for _name, _n in (
    ("ax", 3), ("az", 28), ("bz", 7), ("bx", 3),
    ("lc", 1), ("ly", 3), ("ly2", 3), ("lc2", 1),
    ("gp", 32), ("gz", 7), ("gp2", 32),
    ("wa1", 12), ("wb1", 12), ("wa2", 6), ("wb2", 6), ("w3", 14),
    ("wz", 14), ("wa5", 6), ("wb5", 6), ("wa6", 12), ("wb6", 12), ("n", 1),
):
    COUNT[_name], COUNTS[_name] = TOTAL, _n
    TOTAL += _n


def dot(a, b, dims):
    return lax.dot_general(a, b, (dims, ((), ())), precision=HIGH, preferred_element_type=F32)


def split(v):
    hi = v.astype(BF16)
    return hi, (v - hi.astype(F32)).astype(BF16)


def dot3(a, b, dims):
    def one(p, q):
        return lax.dot_general(p, q, (dims, ((), ())), preferred_element_type=F32)

    return one(a[0], b[0]) + (one(a[0], b[1]) + one(a[1], b[0]))


NN, NT = ((1,), (0,)), ((1,), (1,))


def nn(a, b):
    return dot(a, b, ((1,), (0,)))


def nt(a, b):
    return dot(a, b, ((1,), (1,)))


def tn(a, b):
    return dot(a, b, ((0,), (0,)))


def pivots(done, t):
    shape = (8, 2 * BLK)
    top, rest = t[0:8], t[8:]
    row = lax.broadcasted_iota(jnp.int32, shape, 0)
    lane = lax.broadcasted_iota(jnp.int32, shape, 1)
    cols = [jnp.broadcast_to(top[:, k : k + 1], shape) for k in range(8)]
    for k in range(8):
        rs = lax.rsqrt(jnp.broadcast_to(cols[k][k : k + 1, :], shape))
        col = jnp.where(row > k, cols[k] * rs, 0.0)
        own = jnp.broadcast_to(top[k : k + 1, :], shape) * rs
        top = jnp.where(row == k, own, top - col * own)
        for m in range(k + 1, 8):
            cols[m] = cols[m] - col * (jnp.broadcast_to(cols[m][k : k + 1, :], shape) * rs)
    low = jnp.where(lane < BLK - 8 * done, top, 0.0).T
    for k in range(8):
        rest = rest - low[8:BLK, k : k + 1] * top[k : k + 1, :]
    return pltpu.roll(jnp.concatenate([rest, top], axis=0), 2 * BLK - 8, 1)


def cholesky(a_ref, li_ref):
    lane = lax.broadcasted_iota(jnp.int32, (BLK, 2 * BLK), 1)
    row = lax.broadcasted_iota(jnp.int32, (BLK, 2 * BLK), 0)
    for b in range(RANK // BLK):
        r0 = BLK * b
        w0 = 2 * BLK * (b // 2)
        odd = b % 2
        t = a_ref[r0 : r0 + BLK, w0 : w0 + 2 * BLK]
        if odd:
            t = pltpu.roll(t, BLK, 1)
        t = jnp.where(lane < BLK, t, jnp.where(lane - BLK == row, 1.0, 0.0))
        t = lax.fori_loop(0, BLK // 16, pivots, t)
        yield
        t = lax.fori_loop(BLK // 16, BLK // 8, pivots, t)
        yield
        inv = jnp.where(lane < BLK, t, 0.0)
        if odd:
            inv = pltpu.roll(inv, BLK, 1)
        wide = slice(0, 2 * BLK) if b < 2 else slice(0, RANK)
        ul = nn(inv, li_ref[w0 : w0 + 2 * BLK, wide])
        if r0 + BLK < RANK:
            low = slice(0, RANK) if b == 0 else slice(RANK // 2, RANK)
            u = nn(inv, a_ref[w0 : w0 + 2 * BLK, low])
            rows = lax.broadcasted_iota(jnp.int32, (low.stop - low.start, 1), 0) + low.start
            a_ref[low, low] = a_ref[low, low] - tn(u, u)
            old = li_ref[low, wide]
            li_ref[low, wide] = jnp.where(rows >= r0 + BLK, old - tn(u, ul), old)
        li_ref[r0 : r0 + BLK, wide] = ul
        yield


def kernel(
    mom_hbm, grad_hbm, bas_in,
    right_out, ortho_out, norm_out, newb_out,
    buf, gra, bhi, blo, bas, lpart, lrc, lry, left, thi, tlo, gpart, grx, grz, gram, linv,
    w, rla, rlb, ra1, rb1, sa1, sb1, ra2, rb2, s2, r3, wf, nown, nrec,
    lsem, ssem, rsem,
):
    y = lax.axis_index("replica")
    f = lax.axis_index("fsdp")
    core = lax.axis_index("tensor")
    x, z = f // NZ, f % NZ

    def xp(d):
        return (y, lax.rem(x + d + NX, NX) * NZ + z, core)

    def yp(d):
        return (lax.rem(y + d + NY, NY), f, core)

    def zp(d):
        return (y, x * NZ + lax.rem(z + d + NZ, NZ), core)

    cp = (y, f, 1 - core)

    load_m = pltpu.make_async_copy(mom_hbm, buf, lsem.at[0])
    load_g = pltpu.make_async_copy(grad_hbm, gra, lsem.at[1])
    load_m.start()
    load_g.start()

    sent = []

    def make(src, dst, name, n, dev):
        k = COUNT[name] + n
        return pltpu.make_async_remote_copy(
            src_ref=src, dst_ref=dst, send_sem=ssem.at[k], recv_sem=rsem.at[k],
            device_id=dev, device_id_type=MESH,
        )

    def send(*args):
        copy = make(*args)
        copy.start()
        sent.append(copy)
        return copy

    bas[0, x, z] = bas_in[:, :HALF]
    bas[1, x, z] = bas_in[:, HALF:]

    barrier = pltpu.get_barrier_semaphore()
    plane = {}
    for n in range(1, 2 * NX * NY):
        dx, dy, dc = n // 8, n // 2 % NY, n % 2
        plane[n] = (
            lax.rem(x + dx, NX), lax.rem(y + dy, NY), lax.rem(core + dc, 2),
        )

    def pp(n):
        px, py, pc = plane[n]
        return (py, px * NZ + z, pc)

    peers = [zp(d) for d in range(1, NZ)] + [pp(n) for n in plane]
    for dev in peers:
        pl.semaphore_signal(barrier, inc=1, device_id=dev, device_id_type=MESH)
    load_m.wait()
    load_g.wait()

    @pl.loop(0, MB // 16)
    def _(r):
        rows = pl.ds(pl.multiple_of(r * 16, 16), 16)
        hi, lo = split(buf[rows, :] + gra[rows, :].astype(F32))
        bhi[rows, :] = hi
        blo[rows, :] = lo

    pl.semaphore_wait(barrier, len(peers))

    def ring(way, step, i):
        piece = bas.at[0, lax.rem(x - i + NX, NX), lax.rem(z - way * (step - 1) + NZ, NZ)]
        return send(piece, piece, "az", (16 if way < 0 else 0) + (step - 1) * 4 + i, zp(way))

    hops = {}
    mine = bas.at[0, x, z]
    ax = [send(mine, mine, "ax", d - 1, xp(d)) for d in range(1, NX)]
    hops[1, 1, 0] = ring(1, 1, 0)
    hops[-1, 1, 0] = ring(-1, 1, 0)
    mine = bas.at[1, x, z]
    bz = [send(mine, mine, "bz", d - 1, zp(d)) for d in range(1, NZ)]
    for i in range(1, NX):
        ax[i - 1].wait_recv()
        hops[1, 1, i] = ring(1, 1, i)
        hops[-1, 1, i] = ring(-1, 1, i)
    for copy in bz:
        copy.wait_recv()
    mine = bas.at[1, x]
    bx = [send(mine, mine, "bx", d - 1, xp(d)) for d in range(1, NX)]
    for step in range(2, 5):
        for i in range(NX):
            for way in (1, -1):
                if (way, step - 1, i) in hops:
                    hops.pop((way, step - 1, i)).wait_recv()
                if way == 1 or step < 4:
                    hops[way, step, i] = ring(way, step, i)
    for copy in list(hops.values()) + bx:
        copy.wait_recv()

    hm, qm = MB // 2, MB // 8
    own = pl.multiple_of(core * hm, 16)
    other = pl.multiple_of((1 - core) * hm, 16)

    def left_rows(at):
        rows = pl.ds(at, hm)
        for h in range(2):
            for c in range(0, HALF, 512):
                cols = slice(h * HALF + c, h * HALF + c + 512)
                part = split(bas[h, :, :, :, c : c + 512].reshape(RANK, 512))
                part = dot3((bhi[rows, cols], blo[rows, cols]), part, NT)
                lpart[rows, :] = part if h + c == 0 else lpart[rows, :] + part

    left_rows(other)
    lc = send(lpart.at[pl.ds(other, hm)], lrc, "lc", 0, cp)
    left_rows(own)
    lc.wait_recv()
    lpart[pl.ds(own, hm), :] = lpart[pl.ds(own, hm), :] + lrc[...]

    def quarter(q):
        return pl.ds(pl.multiple_of(own + q * qm, 8), qm)

    ly = [
        send(lpart.at[quarter(lax.rem(y + d, NY))], lry.at[d - 1], "ly", d - 1, yp(d))
        for d in range(1, NY)
    ]
    for copy in ly:
        copy.wait_recv()
    left[quarter(y), :] = (lpart[quarter(y), :] + lry[0] + lry[1] + lry[2]) * 0.25
    mine = left.at[quarter(y)]
    ly2 = [send(mine, mine, "ly2", d - 1, yp(d)) for d in range(1, NY)]

    def grows(base, n):
        return pl.ds(pl.multiple_of(base, 8), n)

    gpart[...] = tn(left[quarter(y), :], left[quarter(y), :])
    gp = []
    for n, (px, py, pc) in plane.items():
        part = gpart.at[grows(128 * pc + 32 * py + 8 * px, 8)]
        gp.append(send(part, grx.at[n], "gp", n, pp(n)))

    for copy in ly2:
        copy.wait_recv()
    mine = left.at[pl.ds(own, hm)]
    lc2 = send(mine, mine, "lc2", 0, cp)

    def yrows(q):
        return pl.ds(pl.multiple_of(q * 64, 64), 64)

    def zrows(q):
        return pl.ds(pl.multiple_of(q * 8, 8), 8)

    def turned(at):
        hi, lo = split(left[pl.ds(at, hm), :].T)
        thi[...] = hi
        tlo[...] = lo

    def half_product(at, h, g):
        cols = pl.ds(pl.multiple_of(h * HALF + g * CH, CH), CH)
        rows = pl.ds(at, hm)
        return dot3((thi[...], tlo[...]), (bhi[rows, cols], blo[rows, cols]), NN)

    turned(own)
    for h in range(2):
        for g in range(NX):
            part = half_product(own, h, g)
            w[h, g, 0] = part[:, :LN]
            w[h, g, 1] = part[:, LN:]
    lc2.wait_recv()
    turned(other)

    def product(h, g):
        part = half_product(other, h, g)
        w[h, g, 0] = w[h, g, 0] + part[:, :LN]
        w[h, g, 1] = w[h, g, 1] + part[:, LN:]

    xr, xl, xo = lax.rem(x + 1, NX), lax.rem(x + 3, NX), lax.rem(x + 2, NX)
    yr, yl, yo = (yrows(lax.rem(y + d, NY)) for d in (1, 3, 2))
    me = yrows(y)
    top, low = slice(0, RANK // 2), slice(RANK // 2, RANK)
    one, two = slice(0, NX // 2), slice(NX // 2, NX)
    A, B = {}, {}

    def to(name, store, c, n, src, dst, dev):
        store[name, c, n] = send(src, dst, name, c * (COUNTS[name] // 2) + n, dev)

    def taken(name, store, c, ns):
        for n in ns:
            store[name, c, n].wait_recv()

    product(0, xo)
    for c in range(2):
        to("wa1", A, c, 0, w.at[0, xo, c, top], rla.at[c, 0], xp(1))
        to("wa1", A, c, 1, w.at[0, xo, c, low], rla.at[c, 1], xp(3))
    product(1, 0)
    product(1, 1)
    for c in range(2):
        to("wb1", B, c, 0, w.at[1, one, c, yo], rlb.at[c, 0], yp(1))
        to("wb1", B, c, 2, w.at[1, one, c, yl], rb1.at[c, 1, one], yp(3))
    product(1, 2)
    product(1, 3)
    for c in range(2):
        to("wb1", B, c, 1, w.at[1, two, c, yo], rlb.at[c, 1], yp(3))
        to("wb1", B, c, 3, w.at[1, two, c, yr], rb1.at[c, 0, two], yp(1))
    for copy in gp:
        copy.wait_recv()
    mine = grows(128 * core + 32 * y + 8 * x, 8)
    total = gpart[mine, :]
    for n in plane:
        total = total + grx[n]
    grz[z] = total
    gz = [send(grz.at[z], grz.at[z], "gz", d - 1, zp(d)) for d in range(1, NZ)]

    product(0, xr)
    for c in range(2):
        to("wa1", A, c, 3, w.at[0, xr, c, low], ra1.at[c, 0, low], xp(1))
    product(0, xl)
    for c in range(2):
        to("wa1", A, c, 2, w.at[0, xl, c, top], ra1.at[c, 1, top], xp(3))

    def relay_a(c):
        taken("wa1", A, c, (0, 1))
        w[0, xr, c, top] = w[0, xr, c, top] + rla[c, 0]
        to("wa1", A, c, 4, w.at[0, xr, c, top], ra1.at[c, 0, top], xp(1))
        w[0, xl, c, low] = w[0, xl, c, low] + rla[c, 1]
        to("wa1", A, c, 5, w.at[0, xl, c, low], ra1.at[c, 1, low], xp(3))

    def relay_b(c):
        taken("wb1", B, c, (0, 1))
        w[1, one, c, yr] = w[1, one, c, yr] + rlb[c, 0]
        to("wb1", B, c, 4, w.at[1, one, c, yr], rb1.at[c, 0, one], yp(1))
        w[1, two, c, yl] = w[1, two, c, yl] + rlb[c, 1]
        to("wb1", B, c, 5, w.at[1, two, c, yl], rb1.at[c, 1, two], yp(3))

    for copy in gz:
        copy.wait_recv()
    total = grz[0]
    for k in range(1, NZ):
        total = total + grz[k]
    gram[mine, :] = total
    part = gram.at[mine]
    gp2 = [send(part, part, "gp2", n, pp(n)) for n in plane]
    relay_a(0)
    relay_b(0)
    product(0, x)
    relay_a(1)
    relay_b(1)

    def one_sum(c):
        taken("wa1", A, c, (2, 3, 4, 5))
        sa1[c] = w[0, x, c] + ra1[c, 0] + ra1[c, 1]
        for d in range(1, NY):
            part = sa1.at[c, yrows(lax.rem(y + d, NY))]
            to("wa2", A, c, d - 1, part, ra2.at[c, d - 1], yp(d))
        taken("wb1", B, c, (2, 3, 4, 5))
        for g in range(NX):
            sb1[c, g] = w[1, g, c, me] + rb1[c, 0, g] + rb1[c, 1, g]
        for d in range(1, NX):
            to("wb2", B, c, d - 1, sb1.at[c, lax.rem(x + d, NX)], rb2.at[c, d - 1], xp(d))

    def two_sum(c):
        taken("wa2", A, c, range(3))
        s2[c, 0] = sa1[c, me] + ra2[c, 0] + ra2[c, 1] + ra2[c, 2]
        taken("wb2", B, c, range(3))
        s2[c, 1] = sb1[c, x] + rb2[c, 0] + rb2[c, 1] + rb2[c, 2]
        for d in range(1, NZ):
            part = s2.at[c, :, zrows(lax.rem(z + d, NZ))]
            to("w3", A, c, d - 1, part, r3.at[c, d - 1], zp(d))

    def three_sum(c):
        taken("w3", A, c, range(7))
        total = s2[c, :, zrows(z)]
        for k in range(NZ - 1):
            total = total + r3[c, k]
        mine = pl.ds(pl.multiple_of(y * 64 + z * 8, 8), 8)
        wf[:, x, c, mine] = total
        part = wf.at[:, x, c, mine]
        for d in range(1, NZ):
            to("wz", A, c, d - 1, part, part, zp(d))

    def four_spread(c):
        taken("wz", A, c, range(7))
        for d in range(1, NY):
            to("wa5", A, c, d - 1, wf.at[0, x, c, me], wf.at[0, x, c, me], yp(d))
        for d in range(1, NX):
            to("wb5", B, c, d - 1, wf.at[1, x, c, me], wf.at[1, x, c, me], xp(d))

    def spread(name, store, c, n, part, dev):
        to(name, store, c, n, part, part, dev)

    def five_spread(c):
        taken("wa5", A, c, range(3))
        spread("wa6", A, c, 0, wf.at[0, x, c, top], xp(1))
        spread("wa6", A, c, 1, wf.at[0, x, c, low], xp(3))
        spread("wa6", A, c, 2, wf.at[0, x, c, low], xp(1))
        spread("wa6", A, c, 3, wf.at[0, x, c, top], xp(3))
        taken("wb5", B, c, range(3))
        spread("wb6", B, c, 0, wf.at[1, one, c, me], yp(1))
        spread("wb6", B, c, 1, wf.at[1, two, c, me], yp(3))
        spread("wb6", B, c, 2, wf.at[1, two, c, me], yp(1))
        spread("wb6", B, c, 3, wf.at[1, one, c, me], yp(3))

    def six_pass(c):
        taken("wa6", A, c, (0, 1))
        spread("wa6", A, c, 4, wf.at[0, xl, c, top], xp(1))
        spread("wa6", A, c, 5, wf.at[0, xr, c, low], xp(3))
        taken("wb6", B, c, (0, 1))
        spread("wb6", B, c, 4, wf.at[1, one, c, yl], yp(1))
        spread("wb6", B, c, 5, wf.at[1, two, c, yr], yp(3))

    one_sum(0)
    for copy in gp2:
        copy.wait_recv()
    for copy in gp2:
        copy.wait_send()
    sent[:] = [copy for copy in sent if not any(copy is c for c in gp2)]
    rows = lax.broadcasted_iota(jnp.int32, (RANK, RANK), 0)
    cols = lax.broadcasted_iota(jnp.int32, (RANK, RANK), 1)
    linv[...] = jnp.where(rows == cols, 1.0, 0.0)
    parts = cholesky(gram, linv)

    def work(step):
        for _ in range(SCHEDULE[step]):
            next(parts, None)

    work(0)
    one_sum(1)
    two_sum(0)
    work(1)
    two_sum(1)
    three_sum(0)
    work(2)
    three_sum(1)
    four_spread(0)
    work(3)
    four_spread(1)
    five_spread(0)
    work(4)
    five_spread(1)
    six_pass(0)
    work(5)
    six_pass(1)

    for _ in parts:
        pass
    li = split(linv[...])
    ortho_out[...] = dot3(split(left[...]), li, NT)
    li = split(linv[...] * 0.25)
    for c in range(2):
        taken("wa6", A, c, (2, 3, 4, 5))
        taken("wb6", B, c, (2, 3, 4, 5))

    nown[...] = jnp.zeros_like(nown)
    for h in range(2):

        @pl.loop(0, NX)
        def _(g):
            part = jnp.concatenate([wf[h, g, 0], wf[h, g, 1]], axis=1)
            part = dot3(li, split(part), NN)
            right_out[:, pl.ds(pl.multiple_of(h * HALF + g * CH, CH), CH)] = part
            sq = part * part
            nown[...] += sq[:, :128] + sq[:, 128:]

    ns = send(nown, nrec, "n", 0, cp)
    ns.wait_recv()
    norms = jnp.sqrt(jnp.sum(nown[...] + nrec[...], axis=1, keepdims=True) + 1e-06)
    norm_out[...] = jnp.broadcast_to(norms, (RANK, 128))
    mine = pl.ds(pl.multiple_of(f * 8, 8), 8)
    newb_out[...] = right_out[mine, :] / norm_out[mine, 0:1]

    for copy in sent:
        copy.wait_send()


def factors(momentum, grad, basis_t):
    v = pltpu.VMEM
    any_ = pl.BlockSpec(memory_space=pltpu.HBM)
    vm = pl.BlockSpec(memory_space=pltpu.VMEM)
    return pl.pallas_call(
        kernel,
        out_shape=(
            jax.ShapeDtypeStruct((RANK, NB), F32),
            jax.ShapeDtypeStruct((MB, RANK), F32),
            jax.ShapeDtypeStruct((RANK, 128), F32),
            jax.ShapeDtypeStruct((8, NB), F32),
        ),
        in_specs=[any_, any_, vm],
        out_specs=(vm, vm, vm, vm),
        scratch_shapes=[
            v((MB, NB), F32), v((MB, NB), BF16), v((MB, NB), BF16), v((MB, NB), BF16),
            v((2, NX, NZ, 8, HALF), F32),
            v((MB, RANK), F32), v((MB // 2, RANK), F32), v((3, MB // 8, RANK), F32),
            v((MB, RANK), F32), v((RANK, MB // 2), BF16), v((RANK, MB // 2), BF16),
            v((RANK, RANK), F32), v((32, 8, RANK), F32), v((NZ, 8, RANK), F32),
            v((RANK, RANK), F32), v((RANK, RANK), F32),
            v((2, NX, 2, RANK, LN), F32),
            v((2, 2, RANK // 2, LN), F32), v((2, 2, NX // 2, 64, LN), F32),
            v((2, 2, RANK, LN), F32), v((2, 2, NX, 64, LN), F32),
            v((2, RANK, LN), F32), v((2, NX, 64, LN), F32),
            v((2, 3, 64, LN), F32), v((2, 3, 64, LN), F32), v((2, 2, 64, LN), F32),
            v((2, 7, 2, 8, LN), F32), v((2, NX, 2, RANK, LN), F32),
            v((RANK, 128), F32), v((RANK, 128), F32),
            pltpu.SemaphoreType.DMA((2,)),
            pltpu.SemaphoreType.DMA((TOTAL,)),
            pltpu.SemaphoreType.DMA((TOTAL,)),
        ],
        compiler_params=pltpu.CompilerParams(
            collective_id=0, has_side_effects=True, vmem_limit_bytes=48 * 1024 * 1024
        ),
        name="factors",
    )(momentum, grad, basis_t)


def update_kernel(ortho, right, norm, mom, grad, weight, new_mom, new_w, ohi, olo):
    @pl.when(pl.program_id(0) == 0)
    def _():
        ohi[...], olo[...] = split(ortho[...])

    scale = 0.1 * math.sqrt(ROWS / COLS)
    part = right[...]
    buffer = mom[...] + grad[...].astype(F32)
    step = jnp.dot(ohi[...], part.astype(BF16), preferred_element_type=F32)
    new_mom[...] = buffer - 0.05 * step
    delta = dot3((ohi[...], olo[...]), split(part / norm[:, 0:1]), NN)
    new_w[...] = (weight[...].astype(F32) - scale * delta).astype(BF16)


def update(ortho, right, norm, momentum, grad, weight):
    cols = pl.BlockSpec((MB, CH), lambda i: (0, i))
    return pl.pallas_call(
        update_kernel,
        grid=(NB // CH,),
        out_shape=(
            jax.ShapeDtypeStruct((MB, NB), F32),
            jax.ShapeDtypeStruct((MB, NB), jnp.bfloat16),
        ),
        in_specs=[
            pl.BlockSpec((MB, RANK), lambda i: (0, 0)),
            pl.BlockSpec((RANK, CH), lambda i: (0, i)),
            pl.BlockSpec((RANK, 128), lambda i: (0, 0)),
            cols, cols, cols,
        ],
        out_specs=(cols, cols),
        scratch_shapes=[pltpu.VMEM((MB, RANK), BF16), pltpu.VMEM((MB, RANK), BF16)],
        compiler_params=pltpu.CompilerParams(vmem_limit_bytes=32 * 1024 * 1024),
        name="update",
    )(ortho, right, norm, momentum, grad, weight)


def body(weight, momentum, grad, basis):
    right, ortho, norm, new_basis_t = factors(momentum[0], grad[0], basis.T)
    new_momentum, new_weight = update(ortho, right, norm, momentum[0], grad[0], weight)
    return new_weight, new_momentum[None], new_basis_t.T


def solution(mesh):
    return jax.shard_map(
        body,
        mesh=mesh,
        in_specs=(
            P("fsdp", "tensor"),
            P("replica", "fsdp", "tensor"),
            P("replica", "fsdp", "tensor"),
            P("tensor", "fsdp"),
        ),
        out_specs=(P("fsdp", "tensor"), P("replica", "fsdp", "tensor"), P("tensor", "fsdp")),
        check_vma=False,
    )
```

```python
import math

import jax
import jax.numpy as jnp
from jax import lax
from jax.experimental import pallas as pl
from jax.experimental.pallas import tpu as pltpu
from jax.sharding import PartitionSpec as P

ROWS = 14336
COLS = 4096
RANK = 256
NX, NY, NZ = 4, 4, 8
MB = 448
NB = 2048
HALF = NB // 2
CH = 256
LN = CH // 2
BLK = 64
MESH = pl.DeviceIdType.MESH
HIGH = lax.Precision.HIGHEST
F32 = jnp.float32
BF16 = jnp.bfloat16
SCHEDULE = (1, 2, 2, 2, 2, 2)

COUNT, COUNTS = {}, {}
TOTAL = 0
for _name, _n in (
    ("ax", 3), ("az", 28), ("bz", 7), ("bx", 32),
    ("lc", 1), ("ly", 3), ("ly2", 3), ("lc2", 1),
    ("gp", 32), ("gz", 7), ("gp2", 32),
    ("wa1", 12), ("wb1", 12), ("wa2", 6), ("wb2", 6), ("w3", 14),
    ("wz", 14), ("wa5", 6), ("wb5", 6), ("wa6", 12), ("wb6", 12), ("n", 1),
):
    COUNT[_name], COUNTS[_name] = TOTAL, _n
    TOTAL += _n


def dot(a, b, dims):
    return lax.dot_general(a, b, (dims, ((), ())), precision=HIGH, preferred_element_type=F32)


def split(v):
    hi = v.astype(BF16)
    return hi, (v - hi.astype(F32)).astype(BF16)


def dot3(a, b, dims):
    def one(p, q):
        return lax.dot_general(p, q, (dims, ((), ())), preferred_element_type=F32)

    return one(a[0], b[0]) + (one(a[0], b[1]) + one(a[1], b[0]))


NN, NT = ((1,), (0,)), ((1,), (1,))


def nn(a, b):
    return dot(a, b, ((1,), (0,)))


def nt(a, b):
    return dot(a, b, ((1,), (1,)))


def tn(a, b):
    return dot(a, b, ((0,), (0,)))


def pivots(done, t):
    shape = (8, 2 * BLK)
    top, rest = t[0:8], t[8:]
    row = lax.broadcasted_iota(jnp.int32, shape, 0)
    lane = lax.broadcasted_iota(jnp.int32, shape, 1)
    cols = [jnp.broadcast_to(top[:, k : k + 1], shape) for k in range(8)]
    for k in range(8):
        rs = lax.rsqrt(jnp.broadcast_to(cols[k][k : k + 1, :], shape))
        col = jnp.where(row > k, cols[k] * rs, 0.0)
        own = jnp.broadcast_to(top[k : k + 1, :], shape) * rs
        top = jnp.where(row == k, own, top - col * own)
        for m in range(k + 1, 8):
            cols[m] = cols[m] - col * (jnp.broadcast_to(cols[m][k : k + 1, :], shape) * rs)
    low = jnp.where(lane < BLK - 8 * done, top, 0.0).T
    for k in range(8):
        rest = rest - low[8:BLK, k : k + 1] * top[k : k + 1, :]
    return pltpu.roll(jnp.concatenate([rest, top], axis=0), 2 * BLK - 8, 1)


def cholesky(a_ref, li_ref):
    lane = lax.broadcasted_iota(jnp.int32, (BLK, 2 * BLK), 1)
    row = lax.broadcasted_iota(jnp.int32, (BLK, 2 * BLK), 0)
    for b in range(RANK // BLK):
        r0 = BLK * b
        w0 = 2 * BLK * (b // 2)
        odd = b % 2
        t = a_ref[r0 : r0 + BLK, w0 : w0 + 2 * BLK]
        if odd:
            t = pltpu.roll(t, BLK, 1)
        t = jnp.where(lane < BLK, t, jnp.where(lane - BLK == row, 1.0, 0.0))
        t = lax.fori_loop(0, BLK // 16, pivots, t)
        yield
        t = lax.fori_loop(BLK // 16, BLK // 8, pivots, t)
        yield
        inv = jnp.where(lane < BLK, t, 0.0)
        if odd:
            inv = pltpu.roll(inv, BLK, 1)
        wide = slice(0, 2 * BLK) if b < 2 else slice(0, RANK)
        ul = nn(inv, li_ref[w0 : w0 + 2 * BLK, wide])
        if r0 + BLK < RANK:
            low = slice(0, RANK) if b == 0 else slice(RANK // 2, RANK)
            u = nn(inv, a_ref[w0 : w0 + 2 * BLK, low])
            rows = lax.broadcasted_iota(jnp.int32, (low.stop - low.start, 1), 0) + low.start
            a_ref[low, low] = a_ref[low, low] - tn(u, u)
            old = li_ref[low, wide]
            li_ref[low, wide] = jnp.where(rows >= r0 + BLK, old - tn(u, ul), old)
        li_ref[r0 : r0 + BLK, wide] = ul
        yield


def kernel(
    mom_hbm, grad_hbm, bas_hbm,
    rhi_out, rlo_out, ortho_out, norm_out, newb_out,
    buf, gra, bas_in, right, bhi, blo, bas, lpart, lrc, lry, left, thi, tlo, gpart, grx, grz, gram, linv,
    w, rla, rlb, ra1, rb1, sa1, sb1, ra2, rb2, s2, r3, wf, nown, nrec,
    lsem, ssem, rsem,
):
    y = lax.axis_index("replica")
    f = lax.axis_index("fsdp")
    core = lax.axis_index("tensor")
    x, z = f // NZ, f % NZ

    def xp(d):
        return (y, lax.rem(x + d + NX, NX) * NZ + z, core)

    def yp(d):
        return (lax.rem(y + d + NY, NY), f, core)

    def zp(d):
        return (y, x * NZ + lax.rem(z + d + NZ, NZ), core)

    cp = (y, f, 1 - core)

    load_m = pltpu.make_async_copy(mom_hbm, buf, lsem.at[0])
    load_g = pltpu.make_async_copy(grad_hbm, gra, lsem.at[1])
    load_b = pltpu.make_async_copy(bas_hbm, bas_in, lsem.at[2])
    load_b.start()
    load_m.start()
    load_g.start()

    sent = []

    def make(src, dst, name, n, dev):
        k = COUNT[name] + n
        return pltpu.make_async_remote_copy(
            src_ref=src, dst_ref=dst, send_sem=ssem.at[k], recv_sem=rsem.at[k],
            device_id=dev, device_id_type=MESH,
        )

    def send(*args):
        copy = make(*args)
        copy.start()
        sent.append(copy)
        return copy

    barrier = pltpu.get_barrier_semaphore()
    plane = {}
    for n in range(1, 2 * NX * NY):
        dx, dy, dc = n // 8, n // 2 % NY, n % 2
        plane[n] = (
            lax.rem(x + dx, NX), lax.rem(y + dy, NY), lax.rem(core + dc, 2),
        )

    def pp(n):
        px, py, pc = plane[n]
        return (py, px * NZ + z, pc)

    peers = [xp(d) for d in range(1, NX)] + [yp(d) for d in range(1, NY)] + [zp(1), zp(-1), cp]
    for dev in peers:
        pl.semaphore_signal(barrier, inc=1, device_id=dev, device_id_type=MESH)
    load_b.wait()
    bas[0, x, z] = bas_in[:, :HALF]
    bas[1, x, z] = bas_in[:, HALF:]
    load_m.wait()
    load_g.wait()

    @pl.loop(0, MB // 16)
    def _(r):
        rows = pl.ds(pl.multiple_of(r * 16, 16), 16)
        hi, lo = split(buf[rows, :] + gra[rows, :].astype(F32))
        bhi[rows, :] = hi
        blo[rows, :] = lo

    pl.semaphore_wait(barrier, len(peers))

    def ring(way, step, i):
        piece = bas.at[0, lax.rem(x - i + NX, NX), lax.rem(z - way * (step - 1) + NZ, NZ)]
        return send(piece, piece, "az", (16 if way < 0 else 0) + (step - 1) * 4 + i, zp(way))

    def across(way, step):
        n = step + (3 if way < 0 else 0)
        piece = bas.at[1, x, lax.rem(z - way * step + NZ, NZ)]
        for k, d in ((0, 1), (1, 3)):
            hops["bx", n, k] = send(piece, piece, "bx", 4 * n + k, xp(d))

    def pass_on(way, step):
        n = step + (3 if way < 0 else 0)
        at = lax.rem(z - way * step + NZ, NZ)
        for k, d, src in ((0, 1, lax.rem(x + 3, NX)), (1, 3, lax.rem(x + 1, NX))):
            hops.pop(("bx", n, k)).wait_recv()
            piece = bas.at[1, src, at, :, k * 512 : k * 512 + 512]
            hops["bx", n, k + 2] = send(piece, piece, "bx", 4 * n + k + 2, xp(d))

    def ring_b(way, step):
        piece = bas.at[1, x, lax.rem(z - way * (step - 1) + NZ, NZ)]
        n = step - 1 + (3 if way < 0 else 0)
        hops["bz", way, step] = send(piece, piece, "bz", n, zp(way))

    hops = {}
    mine = bas.at[0, x, z]
    ax = [send(mine, mine, "ax", d - 1, xp(d)) for d in range(1, NX)]
    hops[1, 1, 0] = ring(1, 1, 0)
    hops[-1, 1, 0] = ring(-1, 1, 0)
    ring_b(1, 1)
    ring_b(-1, 1)
    across(1, 0)
    for i in range(1, NX):
        ax[i - 1].wait_recv()
        hops[1, 1, i] = ring(1, 1, i)
        hops[-1, 1, i] = ring(-1, 1, i)
    for step in range(1, 5):
        for way in (-1, 1):
            if ("bz", way, step) in hops:
                hops.pop(("bz", way, step)).wait_recv()
                if step < (3 if way == 1 else 4):
                    ring_b(way, step + 1)
                across(way, step)
        for i in range(NX):
            for way in (1, -1):
                if (way, step, i) in hops and step < (4 if way == 1 else 3):
                    hops.pop((way, step, i)).wait_recv()
                    hops[way, step + 1, i] = ring(way, step + 1, i)
        if step == 1:
            pass_on(1, 0)
        else:
            pass_on(1, step - 1)
            pass_on(-1, step - 1)
    pass_on(-1, 4)
    for copy in hops.values():
        copy.wait_recv()

    hm, qm = MB // 2, MB // 8
    own = pl.multiple_of(core * hm, 16)
    other = pl.multiple_of((1 - core) * hm, 16)

    def left_rows(at):
        rows = pl.ds(at, hm)
        for h in range(2):
            for c in range(0, HALF, 512):
                cols = slice(h * HALF + c, h * HALF + c + 512)
                part = split(bas[h, :, :, :, c : c + 512].reshape(RANK, 512))
                part = dot3((bhi[rows, cols], blo[rows, cols]), part, NT)
                lpart[rows, :] = part if h + c == 0 else lpart[rows, :] + part

    left_rows(other)
    lc = send(lpart.at[pl.ds(other, hm)], lrc, "lc", 0, cp)
    left_rows(own)
    lc.wait_recv()
    lpart[pl.ds(own, hm), :] = lpart[pl.ds(own, hm), :] + lrc[...]

    def quarter(q):
        return pl.ds(pl.multiple_of(own + q * qm, 8), qm)

    ly = [
        send(lpart.at[quarter(lax.rem(y + d, NY))], lry.at[d - 1], "ly", d - 1, yp(d))
        for d in range(1, NY)
    ]
    for copy in ly:
        copy.wait_recv()
    left[quarter(y), :] = (lpart[quarter(y), :] + lry[0] + lry[1] + lry[2]) * 0.25
    mine = left.at[quarter(y)]
    ly2 = [send(mine, mine, "ly2", d - 1, yp(d)) for d in range(1, NY)]

    def grows(base, n):
        return pl.ds(pl.multiple_of(base, 8), n)

    gpart[...] = tn(left[quarter(y), :], left[quarter(y), :])
    gp = []
    for n, (px, py, pc) in plane.items():
        part = gpart.at[grows(128 * pc + 32 * py + 8 * px, 8)]
        gp.append(send(part, grx.at[n], "gp", n, pp(n)))

    for copy in ly2:
        copy.wait_recv()
    mine = left.at[pl.ds(own, hm)]
    lc2 = send(mine, mine, "lc2", 0, cp)

    def yrows(q):
        return pl.ds(pl.multiple_of(q * 64, 64), 64)

    def zrows(q):
        return pl.ds(pl.multiple_of(q * 8, 8), 8)

    def turned(at):
        hi, lo = split(left[pl.ds(at, hm), :].T)
        thi[...] = hi
        tlo[...] = lo

    def half_product(at, h, g):
        cols = pl.ds(pl.multiple_of(h * HALF + g * CH, CH), CH)
        rows = pl.ds(at, hm)
        return dot3((thi[...], tlo[...]), (bhi[rows, cols], blo[rows, cols]), NN)

    turned(own)
    for h in range(2):
        for g in range(NX):
            part = half_product(own, h, g)
            w[h, g, 0] = part[:, :LN]
            w[h, g, 1] = part[:, LN:]
    lc2.wait_recv()
    turned(other)

    def product(h, g):
        part = half_product(other, h, g)
        w[h, g, 0] = w[h, g, 0] + part[:, :LN]
        w[h, g, 1] = w[h, g, 1] + part[:, LN:]

    xr, xl, xo = lax.rem(x + 1, NX), lax.rem(x + 3, NX), lax.rem(x + 2, NX)
    yr, yl, yo = (yrows(lax.rem(y + d, NY)) for d in (1, 3, 2))
    me = yrows(y)
    top, low = slice(0, RANK // 2), slice(RANK // 2, RANK)
    one, two = slice(0, NX // 2), slice(NX // 2, NX)
    A, B = {}, {}

    def to(name, store, c, n, src, dst, dev):
        store[name, c, n] = send(src, dst, name, c * (COUNTS[name] // 2) + n, dev)

    def taken(name, store, c, ns):
        for n in ns:
            store[name, c, n].wait_recv()

    product(0, xo)
    for c in range(2):
        to("wa1", A, c, 0, w.at[0, xo, c, top], rla.at[c, 0], xp(1))
        to("wa1", A, c, 1, w.at[0, xo, c, low], rla.at[c, 1], xp(3))
    product(1, 0)
    product(1, 1)
    for c in range(2):
        to("wb1", B, c, 0, w.at[1, one, c, yo], rlb.at[c, 0], yp(1))
        to("wb1", B, c, 2, w.at[1, one, c, yl], rb1.at[c, 1, one], yp(3))
    product(1, 2)
    product(1, 3)
    for c in range(2):
        to("wb1", B, c, 1, w.at[1, two, c, yo], rlb.at[c, 1], yp(3))
        to("wb1", B, c, 3, w.at[1, two, c, yr], rb1.at[c, 0, two], yp(1))
    for copy in gp:
        copy.wait_recv()
    mine = grows(128 * core + 32 * y + 8 * x, 8)
    total = gpart[mine, :]
    for n in plane:
        total = total + grx[n]
    grz[z] = total
    gz = [send(grz.at[z], grz.at[z], "gz", d - 1, zp(d)) for d in range(1, NZ)]

    product(0, xr)
    for c in range(2):
        to("wa1", A, c, 3, w.at[0, xr, c, low], ra1.at[c, 0, low], xp(1))
    product(0, xl)
    for c in range(2):
        to("wa1", A, c, 2, w.at[0, xl, c, top], ra1.at[c, 1, top], xp(3))

    def relay_a(c):
        taken("wa1", A, c, (0, 1))
        w[0, xr, c, top] = w[0, xr, c, top] + rla[c, 0]
        to("wa1", A, c, 4, w.at[0, xr, c, top], ra1.at[c, 0, top], xp(1))
        w[0, xl, c, low] = w[0, xl, c, low] + rla[c, 1]
        to("wa1", A, c, 5, w.at[0, xl, c, low], ra1.at[c, 1, low], xp(3))

    def relay_b(c):
        taken("wb1", B, c, (0, 1))
        w[1, one, c, yr] = w[1, one, c, yr] + rlb[c, 0]
        to("wb1", B, c, 4, w.at[1, one, c, yr], rb1.at[c, 0, one], yp(1))
        w[1, two, c, yl] = w[1, two, c, yl] + rlb[c, 1]
        to("wb1", B, c, 5, w.at[1, two, c, yl], rb1.at[c, 1, two], yp(3))

    for copy in gz:
        copy.wait_recv()
    total = grz[0]
    for k in range(1, NZ):
        total = total + grz[k]
    gram[mine, :] = total
    part = gram.at[mine]
    gp2 = [send(part, part, "gp2", n, pp(n)) for n in plane]
    relay_a(0)
    relay_b(0)
    product(0, x)
    relay_a(1)
    relay_b(1)

    def one_sum(c):
        taken("wa1", A, c, (2, 3, 4, 5))
        sa1[c] = w[0, x, c] + ra1[c, 0] + ra1[c, 1]
        for d in range(1, NY):
            part = sa1.at[c, yrows(lax.rem(y + d, NY))]
            to("wa2", A, c, d - 1, part, ra2.at[c, d - 1], yp(d))
        taken("wb1", B, c, (2, 3, 4, 5))
        for g in range(NX):
            sb1[c, g] = w[1, g, c, me] + rb1[c, 0, g] + rb1[c, 1, g]
        for d in range(1, NX):
            to("wb2", B, c, d - 1, sb1.at[c, lax.rem(x + d, NX)], rb2.at[c, d - 1], xp(d))

    def two_sum(c):
        taken("wa2", A, c, range(3))
        s2[c, 0] = sa1[c, me] + ra2[c, 0] + ra2[c, 1] + ra2[c, 2]
        taken("wb2", B, c, range(3))
        s2[c, 1] = sb1[c, x] + rb2[c, 0] + rb2[c, 1] + rb2[c, 2]
        for d in range(1, NZ):
            part = s2.at[c, :, zrows(lax.rem(z + d, NZ))]
            to("w3", A, c, d - 1, part, r3.at[c, d - 1], zp(d))

    def three_sum(c):
        taken("w3", A, c, range(7))
        total = s2[c, :, zrows(z)]
        for k in range(NZ - 1):
            total = total + r3[c, k]
        mine = pl.ds(pl.multiple_of(y * 64 + z * 8, 8), 8)
        wf[:, x, c, mine] = total
        part = wf.at[:, x, c, mine]
        for d in range(1, NZ):
            to("wz", A, c, d - 1, part, part, zp(d))

    def four_spread(c):
        taken("wz", A, c, range(7))
        for d in range(1, NY):
            to("wa5", A, c, d - 1, wf.at[0, x, c, me], wf.at[0, x, c, me], yp(d))
        for d in range(1, NX):
            to("wb5", B, c, d - 1, wf.at[1, x, c, me], wf.at[1, x, c, me], xp(d))

    def spread(name, store, c, n, part, dev):
        to(name, store, c, n, part, part, dev)

    def five_spread(c):
        taken("wa5", A, c, range(3))
        spread("wa6", A, c, 0, wf.at[0, x, c, top], xp(1))
        spread("wa6", A, c, 1, wf.at[0, x, c, low], xp(3))
        spread("wa6", A, c, 2, wf.at[0, x, c, low], xp(1))
        spread("wa6", A, c, 3, wf.at[0, x, c, top], xp(3))
        taken("wb5", B, c, range(3))
        spread("wb6", B, c, 0, wf.at[1, one, c, me], yp(1))
        spread("wb6", B, c, 1, wf.at[1, two, c, me], yp(3))
        spread("wb6", B, c, 2, wf.at[1, two, c, me], yp(1))
        spread("wb6", B, c, 3, wf.at[1, one, c, me], yp(3))

    def six_pass(c):
        taken("wa6", A, c, (0, 1))
        spread("wa6", A, c, 4, wf.at[0, xl, c, top], xp(1))
        spread("wa6", A, c, 5, wf.at[0, xr, c, low], xp(3))
        taken("wb6", B, c, (0, 1))
        spread("wb6", B, c, 4, wf.at[1, one, c, yl], yp(1))
        spread("wb6", B, c, 5, wf.at[1, two, c, yr], yp(3))

    one_sum(0)
    for copy in gp2:
        copy.wait_recv()
    for copy in gp2:
        copy.wait_send()
    sent[:] = [copy for copy in sent if not any(copy is c for c in gp2)]
    rows = lax.broadcasted_iota(jnp.int32, (RANK, RANK), 0)
    cols = lax.broadcasted_iota(jnp.int32, (RANK, RANK), 1)
    linv[...] = jnp.where(rows == cols, 1.0, 0.0)
    parts = cholesky(gram, linv)

    def work(step):
        for _ in range(SCHEDULE[step]):
            next(parts, None)

    work(0)
    one_sum(1)
    two_sum(0)
    work(1)
    two_sum(1)
    three_sum(0)
    work(2)
    three_sum(1)
    four_spread(0)
    work(3)
    four_spread(1)
    five_spread(0)
    work(4)
    five_spread(1)
    six_pass(0)
    work(5)
    six_pass(1)

    for _ in parts:
        pass
    li = split(linv[...])
    ortho_out[...] = dot3(split(left[...]), li, NT)
    li = split(linv[...] * 0.25)
    nown[...] = jnp.zeros_like(nown)

    def right_part(h, g):
        part = jnp.concatenate([wf[h, g, 0], wf[h, g, 1]], axis=1)
        part = dot3(li, split(part), NN)
        cols = pl.ds(pl.multiple_of(h * HALF + g * CH, CH), CH)
        right[:, cols] = part
        hi, lo = split(part)
        rhi_out[:, cols] = hi
        rlo_out[:, cols] = lo
        sq = part * part
        nown[...] += sq[:, :128] + sq[:, 128:]

    right_part(0, x)
    for c in range(2):
        taken("wa6", A, c, (2, 3))
    right_part(0, xl)
    right_part(0, xr)
    for c in range(2):
        taken("wa6", A, c, (4, 5))
    right_part(0, xo)
    for c in range(2):
        taken("wb6", B, c, (2, 3, 4, 5))
    for g in range(NX):
        right_part(1, g)

    ns = send(nown, nrec, "n", 0, cp)
    ns.wait_recv()
    ns.wait_send()
    sent.pop()
    norms = jnp.sqrt(jnp.sum(nown[...] + nrec[...], axis=1, keepdims=True) + 1e-06)
    norms = jnp.broadcast_to(norms, (RANK, 128))
    nown[...] = norms
    norm_out[...] = norms.T[:8]
    mine = pl.ds(pl.multiple_of(f * 8, 8), 8)
    newb_out[...] = right[mine, :] / nown[mine, 0:1]

    for copy in sent:
        copy.wait_send()


def factors(momentum, grad, basis_t):
    v = pltpu.VMEM
    any_ = pl.BlockSpec(memory_space=pltpu.HBM)
    vm = pl.BlockSpec(memory_space=pltpu.VMEM)
    return pl.pallas_call(
        kernel,
        out_shape=(
            jax.ShapeDtypeStruct((RANK, NB), BF16),
            jax.ShapeDtypeStruct((RANK, NB), BF16),
            jax.ShapeDtypeStruct((MB, RANK), F32),
            jax.ShapeDtypeStruct((8, RANK), F32),
            jax.ShapeDtypeStruct((8, NB), F32),
        ),
        in_specs=[any_, any_, any_],
        out_specs=(vm,) * 5,
        scratch_shapes=[
            v((MB, NB), F32), v((MB, NB), BF16), v((8, NB), F32), v((RANK, NB), F32),
            v((MB, NB), BF16), v((MB, NB), BF16),
            v((2, NX, NZ, 8, HALF), F32),
            v((MB, RANK), F32), v((MB // 2, RANK), F32), v((3, MB // 8, RANK), F32),
            v((MB, RANK), F32), v((RANK, MB // 2), BF16), v((RANK, MB // 2), BF16),
            v((RANK, RANK), F32), v((32, 8, RANK), F32), v((NZ, 8, RANK), F32),
            v((RANK, RANK), F32), v((RANK, RANK), F32),
            v((2, NX, 2, RANK, LN), F32),
            v((2, 2, RANK // 2, LN), F32), v((2, 2, NX // 2, 64, LN), F32),
            v((2, 2, RANK, LN), F32), v((2, 2, NX, 64, LN), F32),
            v((2, RANK, LN), F32), v((2, NX, 64, LN), F32),
            v((2, 3, 64, LN), F32), v((2, 3, 64, LN), F32), v((2, 2, 64, LN), F32),
            v((2, 7, 2, 8, LN), F32), v((2, NX, 2, RANK, LN), F32),
            v((RANK, 128), F32), v((RANK, 128), F32),
            pltpu.SemaphoreType.DMA((3,)),
            pltpu.SemaphoreType.DMA((TOTAL,)),
            pltpu.SemaphoreType.DMA((TOTAL,)),
        ],
        compiler_params=pltpu.CompilerParams(
            collective_id=0, has_side_effects=True, vmem_limit_bytes=48 * 1024 * 1024
        ),
        name="factors",
    )(momentum, grad, basis_t)


def update_kernel(ortho, rhi, rlo, norm, mom, grad, weight, mom_hbm, w_hbm, lhs, mom_v, w_v, sems):
    lhs[:MB], _ = split(ortho[...])
    hi, lo = split(ortho[...] / norm[0:1, :])
    lhs[MB : 2 * MB] = hi
    lhs[2 * MB :] = lo
    scale = 0.1 * math.sqrt(ROWS / COLS)
    copies = []
    for n in range(NB // CH):
        cols = slice(n * CH, n * CH + CH)
        both = jnp.dot(lhs[...], rhi[:, cols], preferred_element_type=F32)
        mom_v[n] = mom[:, cols] + grad[:, cols].astype(F32) - 0.05 * both[:MB]
        copies.append(pltpu.make_async_copy(mom_v.at[n], mom_hbm.at[:, cols], sems.at[2 * n]))
        copies[-1].start()
        rest = jnp.dot(lhs[MB : 2 * MB], rlo[:, cols], preferred_element_type=F32)
        delta = both[MB : 2 * MB] + (both[2 * MB :] + rest)
        w_v[n] = (weight[:, cols].astype(F32) - scale * delta).astype(BF16)
        copies.append(pltpu.make_async_copy(w_v.at[n], w_hbm.at[:, cols], sems.at[2 * n + 1]))
        copies[-1].start()
    for copy in copies:
        copy.wait()


def update(ortho, rhi, rlo, norm, momentum, grad, weight):
    vm = pl.BlockSpec(memory_space=pltpu.VMEM)
    any_ = pl.BlockSpec(memory_space=pltpu.HBM)
    steps = NB // CH
    return pl.pallas_call(
        update_kernel,
        out_shape=(
            jax.ShapeDtypeStruct((MB, NB), F32),
            jax.ShapeDtypeStruct((MB, NB), BF16),
        ),
        in_specs=[vm] * 7,
        out_specs=(any_, any_),
        scratch_shapes=[
            pltpu.VMEM((3 * MB, RANK), BF16),
            pltpu.VMEM((steps, MB, CH), F32),
            pltpu.VMEM((steps, MB, CH), BF16),
            pltpu.SemaphoreType.DMA((2 * steps,)),
        ],
        compiler_params=pltpu.CompilerParams(vmem_limit_bytes=32 * 1024 * 1024),
        name="update",
    )(ortho, rhi, rlo, norm, momentum, grad, weight)


def body(weight, momentum, grad, basis):
    rhi, rlo, ortho, norm, new_basis_t = factors(momentum[0], grad[0], basis.T)
    new_momentum, new_weight = update(ortho, rhi, rlo, norm, momentum[0], grad[0], weight)
    return new_weight, new_momentum[None], new_basis_t.T


def solution(mesh):
    return jax.shard_map(
        body,
        mesh=mesh,
        in_specs=(
            P("fsdp", "tensor"),
            P("replica", "fsdp", "tensor"),
            P("replica", "fsdp", "tensor"),
            P("tensor", "fsdp"),
        ),
        out_specs=(P("fsdp", "tensor"), P("replica", "fsdp", "tensor"), P("tensor", "fsdp")),
        check_vma=False,
    )
```

```python
import math

import jax
import jax.numpy as jnp
from jax import lax
from jax.experimental import pallas as pl
from jax.experimental.pallas import tpu as pltpu
from jax.sharding import PartitionSpec as P

ROWS = 14336
COLS = 4096
RANK = 256
NX, NY, NZ = 4, 4, 8
MB = 448
NB = 2048
HALF = NB // 2
CH = 256
LN = CH // 2
BLK = 64
MESH = pl.DeviceIdType.MESH
HIGH = lax.Precision.HIGHEST
F32 = jnp.float32
BF16 = jnp.bfloat16
SCHEDULE = (1, 2, 2, 2, 2, 2)

COUNT, COUNTS = {}, {}
TOTAL = 0
for _name, _n in (
    ("ax", 3), ("az", 28), ("bz", 7), ("bx", 32),
    ("lc", 1), ("ly", 3), ("ly2", 3), ("lc2", 1),
    ("gp", 32), ("gz", 7), ("gp2", 32),
    ("wa1", 12), ("wb1", 12), ("wa2", 6), ("wb2", 6), ("w3", 14),
    ("wz", 14), ("wa5", 6), ("wb5", 6), ("wa6", 12), ("wb6", 12), ("n", 1),
):
    COUNT[_name], COUNTS[_name] = TOTAL, _n
    TOTAL += _n


def dot(a, b, dims):
    return lax.dot_general(a, b, (dims, ((), ())), precision=HIGH, preferred_element_type=F32)


def split(v):
    hi = v.astype(BF16)
    return hi, (v - hi.astype(F32)).astype(BF16)


def dot3(a, b, dims):
    def one(p, q):
        return lax.dot_general(p, q, (dims, ((), ())), preferred_element_type=F32)

    return one(a[0], b[0]) + (one(a[0], b[1]) + one(a[1], b[0]))


NN, NT = ((1,), (0,)), ((1,), (1,))


def nn(a, b):
    return dot(a, b, ((1,), (0,)))


def nt(a, b):
    return dot(a, b, ((1,), (1,)))


def tn(a, b):
    return dot(a, b, ((0,), (0,)))


def pivots(done, t):
    shape = (8, 2 * BLK)
    top, rest = t[0:8], t[8:]
    row = lax.broadcasted_iota(jnp.int32, shape, 0)
    lane = lax.broadcasted_iota(jnp.int32, shape, 1)
    cols = [jnp.broadcast_to(top[:, k : k + 1], shape) for k in range(8)]
    for k in range(8):
        rs = lax.rsqrt(jnp.broadcast_to(cols[k][k : k + 1, :], shape))
        col = jnp.where(row > k, cols[k] * rs, 0.0)
        own = jnp.broadcast_to(top[k : k + 1, :], shape) * rs
        top = jnp.where(row == k, own, top - col * own)
        for m in range(k + 1, 8):
            cols[m] = cols[m] - col * (jnp.broadcast_to(cols[m][k : k + 1, :], shape) * rs)
    low = jnp.where(lane < BLK - 8 * done, top, 0.0).T
    for k in range(8):
        rest = rest - low[8:BLK, k : k + 1] * top[k : k + 1, :]
    return pltpu.roll(jnp.concatenate([rest, top], axis=0), 2 * BLK - 8, 1)


def cholesky(a_ref, li_ref):
    lane = lax.broadcasted_iota(jnp.int32, (BLK, 2 * BLK), 1)
    row = lax.broadcasted_iota(jnp.int32, (BLK, 2 * BLK), 0)
    for b in range(RANK // BLK):
        r0 = BLK * b
        w0 = 2 * BLK * (b // 2)
        odd = b % 2
        t = a_ref[r0 : r0 + BLK, w0 : w0 + 2 * BLK]
        if odd:
            t = pltpu.roll(t, BLK, 1)
        t = jnp.where(lane < BLK, t, jnp.where(lane - BLK == row, 1.0, 0.0))
        t = lax.fori_loop(0, BLK // 16, pivots, t)
        yield
        t = lax.fori_loop(BLK // 16, BLK // 8, pivots, t)
        yield
        inv = jnp.where(lane < BLK, t, 0.0)
        if odd:
            inv = pltpu.roll(inv, BLK, 1)
        wide = slice(0, 2 * BLK) if b < 2 else slice(0, RANK)
        ul = nn(inv, li_ref[w0 : w0 + 2 * BLK, wide])
        if r0 + BLK < RANK:
            low = slice(0, RANK) if b == 0 else slice(RANK // 2, RANK)
            u = nn(inv, a_ref[w0 : w0 + 2 * BLK, low])
            rows = lax.broadcasted_iota(jnp.int32, (low.stop - low.start, 1), 0) + low.start
            a_ref[low, low] = a_ref[low, low] - tn(u, u)
            old = li_ref[low, wide]
            li_ref[low, wide] = jnp.where(rows >= r0 + BLK, old - tn(u, ul), old)
        li_ref[r0 : r0 + BLK, wide] = ul
        yield


def kernel(
    mom_hbm, grad_hbm, bas_hbm,
    rhi_out, rlo_out, ortho_out, norm_out, newb_out,
    buf, gra, bas_in, right, bhi, blo, bas, lpart, lrc, lry, left, thi, tlo, gpart, grx, grz, gram, linv,
    w, rla, rlb, ra1, rb1, sa1, sb1, ra2, rb2, s2, r3, wf, nown, nrec,
    lsem, ssem, rsem,
):
    y = lax.axis_index("replica")
    f = lax.axis_index("fsdp")
    core = lax.axis_index("tensor")
    x, z = f // NZ, f % NZ

    def xp(d):
        return (y, lax.rem(x + d + NX, NX) * NZ + z, core)

    def yp(d):
        return (lax.rem(y + d + NY, NY), f, core)

    def zp(d):
        return (y, x * NZ + lax.rem(z + d + NZ, NZ), core)

    cp = (y, f, 1 - core)

    load_m = pltpu.make_async_copy(mom_hbm, buf, lsem.at[0])
    load_g = pltpu.make_async_copy(grad_hbm, gra, lsem.at[1])
    load_b = pltpu.make_async_copy(bas_hbm, bas_in, lsem.at[2])
    load_b.start()
    load_m.start()
    load_g.start()

    sent = []

    def make(src, dst, name, n, dev):
        k = COUNT[name] + n
        return pltpu.make_async_remote_copy(
            src_ref=src, dst_ref=dst, send_sem=ssem.at[k], recv_sem=rsem.at[k],
            device_id=dev, device_id_type=MESH,
        )

    def send(*args):
        copy = make(*args)
        copy.start()
        sent.append(copy)
        return copy

    barrier = pltpu.get_barrier_semaphore()
    plane = {}
    for n in range(1, 2 * NX * NY):
        dx, dy, dc = n // 8, n // 2 % NY, n % 2
        plane[n] = (
            lax.rem(x + dx, NX), lax.rem(y + dy, NY), lax.rem(core + dc, 2),
        )

    def pp(n):
        px, py, pc = plane[n]
        return (py, px * NZ + z, pc)

    peers = [xp(d) for d in range(1, NX)] + [yp(d) for d in range(1, NY)] + [zp(1), zp(-1), cp]
    for dev in peers:
        pl.semaphore_signal(barrier, inc=1, device_id=dev, device_id_type=MESH)
    load_b.wait()
    bas[0, x, z] = bas_in[:, :HALF]
    bas[1, x, z] = bas_in[:, HALF:]
    load_m.wait()
    load_g.wait()

    @pl.loop(0, MB // 16)
    def _(r):
        rows = pl.ds(pl.multiple_of(r * 16, 16), 16)
        hi, lo = split(buf[rows, :] + gra[rows, :].astype(F32))
        bhi[rows, :] = hi
        blo[rows, :] = lo

    pl.semaphore_wait(barrier, len(peers))

    def ring(way, step, i):
        piece = bas.at[0, lax.rem(x - i + NX, NX), lax.rem(z - way * (step - 1) + NZ, NZ)]
        return send(piece, piece, "az", (16 if way < 0 else 0) + (step - 1) * 4 + i, zp(way))

    def across(way, step):
        n = step + (3 if way < 0 else 0)
        piece = bas.at[1, x, lax.rem(z - way * step + NZ, NZ)]
        for k, d in ((0, 1), (1, 3)):
            hops["bx", n, k] = send(piece, piece, "bx", 4 * n + k, xp(d))

    def pass_on(way, step):
        n = step + (3 if way < 0 else 0)
        at = lax.rem(z - way * step + NZ, NZ)
        for k, d, src in ((0, 1, lax.rem(x + 3, NX)), (1, 3, lax.rem(x + 1, NX))):
            hops.pop(("bx", n, k)).wait_recv()
            piece = bas.at[1, src, at, :, k * 512 : k * 512 + 512]
            hops["bx", n, k + 2] = send(piece, piece, "bx", 4 * n + k + 2, xp(d))

    def ring_b(way, step):
        piece = bas.at[1, x, lax.rem(z - way * (step - 1) + NZ, NZ)]
        n = step - 1 + (3 if way < 0 else 0)
        hops["bz", way, step] = send(piece, piece, "bz", n, zp(way))

    hops = {}
    mine = bas.at[0, x, z]
    ax = [send(mine, mine, "ax", d - 1, xp(d)) for d in range(1, NX)]
    hops[1, 1, 0] = ring(1, 1, 0)
    hops[-1, 1, 0] = ring(-1, 1, 0)
    ring_b(1, 1)
    ring_b(-1, 1)
    across(1, 0)
    for i in range(1, NX):
        ax[i - 1].wait_recv()
        hops[1, 1, i] = ring(1, 1, i)
        hops[-1, 1, i] = ring(-1, 1, i)
    for step in range(1, 5):
        for way in (-1, 1):
            if ("bz", way, step) in hops:
                hops.pop(("bz", way, step)).wait_recv()
                if step < (3 if way == 1 else 4):
                    ring_b(way, step + 1)
                across(way, step)
        for i in range(NX):
            for way in (1, -1):
                if (way, step, i) in hops and step < (4 if way == 1 else 3):
                    hops.pop((way, step, i)).wait_recv()
                    hops[way, step + 1, i] = ring(way, step + 1, i)
        if step == 1:
            pass_on(1, 0)
        else:
            pass_on(1, step - 1)
            pass_on(-1, step - 1)
    pass_on(-1, 4)
    for copy in hops.values():
        copy.wait_recv()

    hm, qm = MB // 2, MB // 8
    own = pl.multiple_of(core * hm, 16)
    other = pl.multiple_of((1 - core) * hm, 16)

    def left_rows(at):
        rows = pl.ds(at, hm)
        for h in range(2):
            for c in range(0, HALF, 512):
                cols = slice(h * HALF + c, h * HALF + c + 512)
                part = split(bas[h, :, :, :, c : c + 512].reshape(RANK, 512))
                part = dot3((bhi[rows, cols], blo[rows, cols]), part, NT)
                lpart[rows, :] = part if h + c == 0 else lpart[rows, :] + part

    left_rows(other)
    lc = send(lpart.at[pl.ds(other, hm)], lrc, "lc", 0, cp)
    left_rows(own)
    lc.wait_recv()
    lpart[pl.ds(own, hm), :] = lpart[pl.ds(own, hm), :] + lrc[...]

    def quarter(q):
        return pl.ds(pl.multiple_of(own + q * qm, 8), qm)

    ly = [
        send(lpart.at[quarter(lax.rem(y + d, NY))], lry.at[d - 1], "ly", d - 1, yp(d))
        for d in range(1, NY)
    ]
    for copy in ly:
        copy.wait_recv()
    left[quarter(y), :] = (lpart[quarter(y), :] + lry[0] + lry[1] + lry[2]) * 0.25
    mine = left.at[quarter(y)]
    ly2 = [send(mine, mine, "ly2", d - 1, yp(d)) for d in range(1, NY)]

    def grows(base, n):
        return pl.ds(pl.multiple_of(base, 8), n)

    gpart[...] = tn(left[quarter(y), :], left[quarter(y), :])
    gp = []
    for n, (px, py, pc) in plane.items():
        part = gpart.at[grows(128 * pc + 32 * py + 8 * px, 8)]
        gp.append(send(part, grx.at[n], "gp", n, pp(n)))

    for copy in ly2:
        copy.wait_recv()
    mine = left.at[pl.ds(own, hm)]
    lc2 = send(mine, mine, "lc2", 0, cp)

    def yrows(q):
        return pl.ds(pl.multiple_of(q * 64, 64), 64)

    def zrows(q):
        return pl.ds(pl.multiple_of(q * 8, 8), 8)

    def turned(at):
        hi, lo = split(left[pl.ds(at, hm), :].T)
        thi[...] = hi
        tlo[...] = lo

    def half_product(at, h, g):
        cols = pl.ds(pl.multiple_of(h * HALF + g * CH, CH), CH)
        rows = pl.ds(at, hm)
        return dot3((thi[...], tlo[...]), (bhi[rows, cols], blo[rows, cols]), NN)

    turned(own)
    for h in range(2):
        for g in range(NX):
            part = half_product(own, h, g)
            w[h, g, 0] = part[:, :LN]
            w[h, g, 1] = part[:, LN:]
    lc2.wait_recv()
    turned(other)

    def product(h, g):
        part = half_product(other, h, g)
        w[h, g, 0] = w[h, g, 0] + part[:, :LN]
        w[h, g, 1] = w[h, g, 1] + part[:, LN:]

    xr, xl, xo = lax.rem(x + 1, NX), lax.rem(x + 3, NX), lax.rem(x + 2, NX)
    yr, yl, yo = (yrows(lax.rem(y + d, NY)) for d in (1, 3, 2))
    me = yrows(y)
    top, low = slice(0, RANK // 2), slice(RANK // 2, RANK)
    one, two = slice(0, NX // 2), slice(NX // 2, NX)
    A, B = {}, {}

    def to(name, store, c, n, src, dst, dev):
        store[name, c, n] = send(src, dst, name, c * (COUNTS[name] // 2) + n, dev)

    def taken(name, store, c, ns):
        for n in ns:
            store[name, c, n].wait_recv()

    product(0, xo)
    for c in range(2):
        to("wa1", A, c, 0, w.at[0, xo, c, top], rla.at[c, 0], xp(1))
        to("wa1", A, c, 1, w.at[0, xo, c, low], rla.at[c, 1], xp(3))
    product(1, 0)
    product(1, 1)
    for c in range(2):
        to("wb1", B, c, 0, w.at[1, one, c, yo], rlb.at[c, 0], yp(1))
        to("wb1", B, c, 2, w.at[1, one, c, yl], rb1.at[c, 1, one], yp(3))
    product(1, 2)
    product(1, 3)
    for c in range(2):
        to("wb1", B, c, 1, w.at[1, two, c, yo], rlb.at[c, 1], yp(3))
        to("wb1", B, c, 3, w.at[1, two, c, yr], rb1.at[c, 0, two], yp(1))
    for copy in gp:
        copy.wait_recv()
    mine = grows(128 * core + 32 * y + 8 * x, 8)
    total = gpart[mine, :]
    for n in plane:
        total = total + grx[n]
    grz[z] = total
    gz = [send(grz.at[z], grz.at[z], "gz", d - 1, zp(d)) for d in range(1, NZ)]

    product(0, xr)
    for c in range(2):
        to("wa1", A, c, 3, w.at[0, xr, c, low], ra1.at[c, 0, low], xp(1))
    product(0, xl)
    for c in range(2):
        to("wa1", A, c, 2, w.at[0, xl, c, top], ra1.at[c, 1, top], xp(3))

    def relay_a(c):
        taken("wa1", A, c, (0, 1))
        w[0, xr, c, top] = w[0, xr, c, top] + rla[c, 0]
        to("wa1", A, c, 4, w.at[0, xr, c, top], ra1.at[c, 0, top], xp(1))
        w[0, xl, c, low] = w[0, xl, c, low] + rla[c, 1]
        to("wa1", A, c, 5, w.at[0, xl, c, low], ra1.at[c, 1, low], xp(3))

    def relay_b(c):
        taken("wb1", B, c, (0, 1))
        w[1, one, c, yr] = w[1, one, c, yr] + rlb[c, 0]
        to("wb1", B, c, 4, w.at[1, one, c, yr], rb1.at[c, 0, one], yp(1))
        w[1, two, c, yl] = w[1, two, c, yl] + rlb[c, 1]
        to("wb1", B, c, 5, w.at[1, two, c, yl], rb1.at[c, 1, two], yp(3))

    for copy in gz:
        copy.wait_recv()
    total = grz[0]
    for k in range(1, NZ):
        total = total + grz[k]
    gram[mine, :] = total
    part = gram.at[mine]
    gp2 = [send(part, part, "gp2", n, pp(n)) for n in plane]
    relay_a(0)
    relay_b(0)
    product(0, x)
    relay_a(1)
    relay_b(1)

    def one_sum(c):
        taken("wa1", A, c, (2, 3, 4, 5))
        sa1[c] = w[0, x, c] + ra1[c, 0] + ra1[c, 1]
        for d in range(1, NY):
            part = sa1.at[c, yrows(lax.rem(y + d, NY))]
            to("wa2", A, c, d - 1, part, ra2.at[c, d - 1], yp(d))
        taken("wb1", B, c, (2, 3, 4, 5))
        for g in range(NX):
            sb1[c, g] = w[1, g, c, me] + rb1[c, 0, g] + rb1[c, 1, g]
        for d in range(1, NX):
            to("wb2", B, c, d - 1, sb1.at[c, lax.rem(x + d, NX)], rb2.at[c, d - 1], xp(d))

    def two_sum(c):
        taken("wa2", A, c, range(3))
        s2[c, 0] = sa1[c, me] + ra2[c, 0] + ra2[c, 1] + ra2[c, 2]
        taken("wb2", B, c, range(3))
        s2[c, 1] = sb1[c, x] + rb2[c, 0] + rb2[c, 1] + rb2[c, 2]
        for d in range(1, NZ):
            part = s2.at[c, :, zrows(lax.rem(z + d, NZ))]
            to("w3", A, c, d - 1, part, r3.at[c, d - 1], zp(d))

    def three_sum(c):
        taken("w3", A, c, range(7))
        total = s2[c, :, zrows(z)]
        for k in range(NZ - 1):
            total = total + r3[c, k]
        mine = pl.ds(pl.multiple_of(y * 64 + z * 8, 8), 8)
        wf[:, x, c, mine] = total
        part = wf.at[:, x, c, mine]
        for d in range(1, NZ):
            to("wz", A, c, d - 1, part, part, zp(d))

    def four_spread(c):
        taken("wz", A, c, range(7))
        for d in range(1, NY):
            to("wa5", A, c, d - 1, wf.at[0, x, c, me], wf.at[0, x, c, me], yp(d))
        for d in range(1, NX):
            to("wb5", B, c, d - 1, wf.at[1, x, c, me], wf.at[1, x, c, me], xp(d))

    def spread(name, store, c, n, part, dev):
        to(name, store, c, n, part, part, dev)

    def five_spread(c):
        taken("wa5", A, c, range(3))
        spread("wa6", A, c, 0, wf.at[0, x, c, top], xp(1))
        spread("wa6", A, c, 1, wf.at[0, x, c, low], xp(3))
        spread("wa6", A, c, 2, wf.at[0, x, c, low], xp(1))
        spread("wa6", A, c, 3, wf.at[0, x, c, top], xp(3))
        taken("wb5", B, c, range(3))
        spread("wb6", B, c, 0, wf.at[1, one, c, me], yp(1))
        spread("wb6", B, c, 1, wf.at[1, two, c, me], yp(3))
        spread("wb6", B, c, 2, wf.at[1, two, c, me], yp(1))
        spread("wb6", B, c, 3, wf.at[1, one, c, me], yp(3))

    def six_pass(c):
        taken("wa6", A, c, (0, 1))
        spread("wa6", A, c, 4, wf.at[0, xl, c, top], xp(1))
        spread("wa6", A, c, 5, wf.at[0, xr, c, low], xp(3))
        taken("wb6", B, c, (0, 1))
        spread("wb6", B, c, 4, wf.at[1, one, c, yl], yp(1))
        spread("wb6", B, c, 5, wf.at[1, two, c, yr], yp(3))

    one_sum(0)
    for copy in gp2:
        copy.wait_recv()
    for copy in gp2:
        copy.wait_send()
    sent[:] = [copy for copy in sent if not any(copy is c for c in gp2)]
    rows = lax.broadcasted_iota(jnp.int32, (RANK, RANK), 0)
    cols = lax.broadcasted_iota(jnp.int32, (RANK, RANK), 1)
    linv[...] = jnp.where(rows == cols, 1.0, 0.0)
    parts = cholesky(gram, linv)

    def work(step):
        for _ in range(SCHEDULE[step]):
            next(parts, None)

    work(0)
    one_sum(1)
    two_sum(0)
    work(1)
    two_sum(1)
    three_sum(0)
    work(2)
    three_sum(1)
    four_spread(0)
    work(3)
    four_spread(1)
    five_spread(0)
    work(4)
    five_spread(1)
    six_pass(0)
    work(5)
    six_pass(1)

    for _ in parts:
        pass
    li = split(linv[...])
    ortho_out[...] = dot3(split(left[...]), li, NT)
    li = split(linv[...] * 0.25)
    nown[...] = jnp.zeros_like(nown)

    def right_part(h, g):
        part = jnp.concatenate([wf[h, g, 0], wf[h, g, 1]], axis=1)
        part = dot3(li, split(part), NN)
        cols = pl.ds(pl.multiple_of(h * HALF + g * CH, CH), CH)
        right[:, cols] = part
        hi, lo = split(part)
        rhi_out[:, cols] = hi
        rlo_out[:, cols] = lo
        sq = part * part
        nown[...] += sq[:, :128] + sq[:, 128:]

    right_part(0, x)
    for c in range(2):
        taken("wa6", A, c, (2, 3))
    right_part(0, xl)
    right_part(0, xr)
    for c in range(2):
        taken("wa6", A, c, (4, 5))
    right_part(0, xo)
    for c in range(2):
        taken("wb6", B, c, (2, 3, 4, 5))
    for g in range(NX):
        right_part(1, g)

    ns = send(nown, nrec, "n", 0, cp)
    ns.wait_recv()
    ns.wait_send()
    sent.pop()
    norms = jnp.sqrt(jnp.sum(nown[...] + nrec[...], axis=1, keepdims=True) + 1e-06)
    norms = jnp.broadcast_to(norms, (RANK, 128))
    nown[...] = norms
    norm_out[...] = norms.T[:8]
    mine = pl.ds(pl.multiple_of(f * 8, 8), 8)
    newb_out[...] = right[mine, :] / nown[mine, 0:1]

    for copy in sent:
        copy.wait_send()


def factors(momentum, grad, basis_t):
    v = pltpu.VMEM
    any_ = pl.BlockSpec(memory_space=pltpu.HBM)
    vm = pl.BlockSpec(memory_space=pltpu.VMEM)
    return pl.pallas_call(
        kernel,
        out_shape=(
            jax.ShapeDtypeStruct((RANK, NB), BF16),
            jax.ShapeDtypeStruct((RANK, NB), BF16),
            jax.ShapeDtypeStruct((MB, RANK), F32),
            jax.ShapeDtypeStruct((8, RANK), F32),
            jax.ShapeDtypeStruct((8, NB), F32),
        ),
        in_specs=[any_, any_, any_],
        out_specs=(vm,) * 5,
        scratch_shapes=[
            v((MB, NB), F32), v((MB, NB), BF16), v((8, NB), F32), v((RANK, NB), F32),
            v((MB, NB), BF16), v((MB, NB), BF16),
            v((2, NX, NZ, 8, HALF), F32),
            v((MB, RANK), F32), v((MB // 2, RANK), F32), v((3, MB // 8, RANK), F32),
            v((MB, RANK), F32), v((RANK, MB // 2), BF16), v((RANK, MB // 2), BF16),
            v((RANK, RANK), F32), v((32, 8, RANK), F32), v((NZ, 8, RANK), F32),
            v((RANK, RANK), F32), v((RANK, RANK), F32),
            v((2, NX, 2, RANK, LN), F32),
            v((2, 2, RANK // 2, LN), F32), v((2, 2, NX // 2, 64, LN), F32),
            v((2, 2, RANK, LN), F32), v((2, 2, NX, 64, LN), F32),
            v((2, RANK, LN), F32), v((2, NX, 64, LN), F32),
            v((2, 3, 64, LN), F32), v((2, 3, 64, LN), F32), v((2, 2, 64, LN), F32),
            v((2, 7, 2, 8, LN), F32), v((2, NX, 2, RANK, LN), F32),
            v((RANK, 128), F32), v((RANK, 128), F32),
            pltpu.SemaphoreType.DMA((3,)),
            pltpu.SemaphoreType.DMA((TOTAL,)),
            pltpu.SemaphoreType.DMA((TOTAL,)),
        ],
        compiler_params=pltpu.CompilerParams(
            collective_id=0, has_side_effects=True, vmem_limit_bytes=48 * 1024 * 1024
        ),
        name="factors",
    )(momentum, grad, basis_t)


def update_kernel(
    ortho, rhi, rlo, norm, newb, mom, grad, weight,
    mom_hbm, w_hbm, newb_hbm, lhs, mom_v, w_v, sems,
):
    copies = [pltpu.make_async_copy(newb, newb_hbm, sems.at[2 * NB // CH])]
    copies[0].start()
    lhs[:MB], _ = split(ortho[...])
    hi, lo = split(ortho[...] / norm[0:1, :])
    lhs[MB : 2 * MB] = hi
    lhs[2 * MB :] = lo
    scale = 0.1 * math.sqrt(ROWS / COLS)
    for n in range(NB // CH):
        cols = slice(n * CH, n * CH + CH)
        both = jnp.dot(lhs[...], rhi[:, cols], preferred_element_type=F32)
        mom_v[n] = mom[:, cols] + grad[:, cols].astype(F32) - 0.05 * both[:MB]
        copies.append(pltpu.make_async_copy(mom_v.at[n], mom_hbm.at[:, cols], sems.at[2 * n]))
        copies[-1].start()
        rest = jnp.dot(lhs[MB : 2 * MB], rlo[:, cols], preferred_element_type=F32)
        delta = both[MB : 2 * MB] + (both[2 * MB :] + rest)
        w_v[n] = (weight[:, cols].astype(F32) - scale * delta).astype(BF16)
        copies.append(pltpu.make_async_copy(w_v.at[n], w_hbm.at[:, cols], sems.at[2 * n + 1]))
        copies[-1].start()
    for copy in copies:
        copy.wait()


def update(ortho, rhi, rlo, norm, newb, momentum, grad, weight):
    vm = pl.BlockSpec(memory_space=pltpu.VMEM)
    any_ = pl.BlockSpec(memory_space=pltpu.HBM)
    steps = NB // CH
    return pl.pallas_call(
        update_kernel,
        out_shape=(
            jax.ShapeDtypeStruct((MB, NB), F32),
            jax.ShapeDtypeStruct((MB, NB), BF16),
            jax.ShapeDtypeStruct((8, NB), F32),
        ),
        in_specs=[vm] * 8,
        out_specs=(any_, any_, any_),
        scratch_shapes=[
            pltpu.VMEM((3 * MB, RANK), BF16),
            pltpu.VMEM((steps, MB, CH), F32),
            pltpu.VMEM((steps, MB, CH), BF16),
            pltpu.SemaphoreType.DMA((2 * steps + 1,)),
        ],
        compiler_params=pltpu.CompilerParams(vmem_limit_bytes=32 * 1024 * 1024),
        name="update",
    )(ortho, rhi, rlo, norm, newb, momentum, grad, weight)


def body(weight, momentum, grad, basis):
    rhi, rlo, ortho, norm, newb = factors(momentum[0], grad[0], basis.T)
    new_momentum, new_weight, new_basis_t = update(
        ortho, rhi, rlo, norm, newb, momentum[0], grad[0], weight
    )
    return new_weight, new_momentum[None], new_basis_t.T


def solution(mesh):
    return jax.shard_map(
        body,
        mesh=mesh,
        in_specs=(
            P("fsdp", "tensor"),
            P("replica", "fsdp", "tensor"),
            P("replica", "fsdp", "tensor"),
            P("tensor", "fsdp"),
        ),
        out_specs=(P("fsdp", "tensor"), P("replica", "fsdp", "tensor"), P("tensor", "fsdp")),
        check_vma=False,
    )
```
